256 devices in a mesh: tile: 16 (over x_hi, y, core), pulse: 16 (over z, x_lo).
Axes of the slice: x: 4 (x_hi: 2, x_lo: 2; x = x_hi * 2 + x_lo), y: 4, z: 8, core: 2. Of those that a mesh axis runs over, the one named last changes fastest.
Arguments:
- pulse_data: bfloat16 [2, 512, 16384], P(None, 'pulse', 'tile'), may hold values from -6 to 6
- phases: float32 [512], P('pulse'), may hold values from -3.140625 to 3.140625
- offsets: int32 [64], replicated, may hold values from -12 to 12
- widths: int32 [64], replicated, may hold values from 1 to 4
- visible: int32 [16, 64], P('tile'), may hold values 0 or 1
- lagged: bfloat16 [2, 8192, 16384], P(None, 'tile', 'pulse'), may hold values from -70 to 70
Outputs:
- image: bfloat16 [2, 8192, 16384], P(None, 'tile', 'pulse')
- phase_gradient: float32 [512], P('pulse')
The draws below stay inside these ranges and needn't reach their ends.
All inputs are finite; a program needn't handle non-finite values. No bound on the sum of `visible` on one device may be relied on, other than what follows from the above.
Results may differ from the reference program's by a relative error of at most 0.0062.
Values may be sent and summed in bfloat16 or wider, within the bound.
No kernel may reach another device: no remote copies, remote signals or barrier semaphores. Data moves between devices by JAX's collectives and lax.ppermute only.
A program may use at most 128 MiB of HBM per device.

```python
import math
import jax
import jax.numpy as jnp
from jax import lax

ROWS_DEV = 512
PB = 8
OFFMAX = 12
WMAX = 4
HALO = 16
ROWS = 8192
COLS = 16384
BINS = 16384
PULSES = 512
NBLK = 64
N_TILE = 16


def draw_lagged(key, part):
    key = jax.random.fold_in(key, 7)
    row_key, col_key, value_key = jax.random.split(key, 3)
    row_pos = jnp.arange(ROWS, dtype=jnp.float32) / ROWS
    row_scale = jnp.exp(jax.random.uniform(row_key, (ROWS,), jnp.float32, -1.15, 1.15) + 1.1 * row_pos - 0.55)
    col_scale = jnp.exp(jax.random.uniform(col_key, (COLS,), jnp.float32, -1.15, 1.15))
    values = jnp.clip(jax.random.normal(value_key, (2, ROWS, COLS), jnp.float32), -4.0, 4.0)
    return (values * row_scale[None, :, None] * col_scale[None, None, :]).astype(jnp.bfloat16)


def touch_ends(result, key, smallest, high):
    spot = [jax.random.randint(jax.random.fold_in(key, axis), (), 0, length) for axis, length in enumerate(result.shape)]
    longest = result.shape.index(max(result.shape))
    beside = spot[:longest] + [(spot[longest] + 1) % result.shape[longest]] + spot[longest + 1:]
    return result.at[tuple(spot)].set(smallest).at[tuple(beside)].set(high)


def level_of(rng, shape, pieces, smallest, high):
    gain = 1.0
    for position, parts in pieces:
        steps = jax.random.uniform(jax.random.fold_in(jax.random.fold_in(rng, 6), position), (parts,), jnp.float32, smallest / len(pieces), high / len(pieces))
        gain = gain * jnp.repeat(jnp.exp(steps), shape[position] // parts).reshape((-1,) + (1,) * (len(shape) - 1 - position))
    return gain


def scatter_about(rng, shape, width, limit, cuts=(), kind=jnp.bfloat16):
    result = jax.random.normal(rng, shape, jnp.float32) * width
    if len(cuts) > 0:
        result = level_of(rng, shape, cuts, -0.22, 0.18) * result
    return jnp.clip(result, min=-limit, max=limit).astype(kind)


def setup_inputs(seed: int = 0) -> dict:
    key_list = jax.random.split(jax.random.key(seed), 7)
    return {
        "pulse_data": scatter_about(key_list[0], (2, PULSES, BINS), 1.0, 6.0, ((1, 16), (2, 16))),
        "phases": jnp.clip(jax.random.uniform(key_list[1], (PULSES,), jnp.float32, -3.140625, 3.140625), -3.140625, 3.140625),
        "offsets": touch_ends(jax.random.randint(key_list[2], (NBLK,), 0 - OFFMAX, OFFMAX + 1), jax.random.fold_in(key_list[2], 1), 0 - OFFMAX, OFFMAX).astype(jnp.int32),
        "widths": touch_ends(jax.random.randint(key_list[3], (NBLK,), 1, WMAX + 1), jax.random.fold_in(key_list[3], 1), 1, WMAX).astype(jnp.int32),
        "visible": touch_ends((jax.random.randint(key_list[4], (N_TILE, NBLK), 0, 4) < 3).astype(jnp.int32), jax.random.fold_in(key_list[4], 1), 0, 1),
        "lagged": draw_lagged(jax.random.fold_in(key_list[6], 71), 0),
    }


def taper_project(window, shifts, spreads, weight):
    count = window.shape[1]
    rows = (window.shape[2] - 2 * HALO) // 2
    centre = 2 * jnp.arange(rows, dtype=jnp.int32)[None, :] + shifts[:, None] + HALO
    breadth = spreads.astype(jnp.float32)
    summed = jnp.zeros((2, count, rows), jnp.float32)
    for tap in range(1 - WMAX, WMAX):
        index = jnp.broadcast_to((centre + tap)[None, :, :], (2, count, rows))
        picked = jnp.take_along_axis(window, index, axis=2).astype(jnp.float32)
        taper = jnp.maximum(breadth - abs(tap), 0.0) / (breadth * breadth)
        summed = summed + taper[None, :, None] * picked
    return (summed * weight[None, :, None]).astype(jnp.bfloat16)

def steering(first_column, column_count, pulse_count, period):
    pulse_index = jnp.arange(pulse_count, dtype=jnp.int32)[:, None]
    column = first_column + jnp.arange(column_count, dtype=jnp.int32)[None, :]
    angle = (pulse_index * column % period).astype(jnp.float32) * (2.0 * math.pi / period)
    return (jnp.cos(angle).astype(jnp.bfloat16), jnp.sin(angle).astype(jnp.bfloat16))

def product(left, right, dims):
    return lax.dot_general(left, right, dims, preferred_element_type=jnp.float32)

def reference(pulse_data, phases, offsets, widths, visible, lagged):
    data_real = pulse_data[0].astype(jnp.float32)
    data_imag = pulse_data[1].astype(jnp.float32)
    cosine = jnp.cos(phases)[:, None]
    sine = jnp.sin(phases)[:, None]
    phased = jnp.stack([data_real * cosine - data_imag * sine, data_real * sine + data_imag * cosine]).astype(jnp.bfloat16)
    padded = jnp.pad(phased, ((0, 0), (0, 0), (HALO, HALO)))
    pulse_block = jnp.arange(PULSES, dtype=jnp.int32) // PB
    shifts = offsets[pulse_block]
    spreads = widths[pulse_block]
    steer_real, steer_imag = steering(0, COLS, PULSES, COLS)
    first = (((0,), (0,)), ((), ()))
    last = (((1,), (1,)), ((), ()))

    def tile_work(tile):
        window = lax.dynamic_slice_in_dim(padded, (tile * 2 * ROWS_DEV).astype(jnp.int32), 2 * ROWS_DEV + 2 * HALO, 2)
        keep = visible[tile][pulse_block].astype(jnp.float32)
        contrib = taper_project(window, shifts, spreads, keep)
        image_real = product(contrib[0], steer_real, first) - product(contrib[1], steer_imag, first)
        image_imag = product(contrib[0], steer_imag, first) + product(contrib[1], steer_real, first)
        part = lax.dynamic_slice_in_dim(lagged, (tile * ROWS_DEV).astype(jnp.int32), ROWS_DEV, 1)
        lag_real = part[0].astype(jnp.float32)
        lag_imag = part[1].astype(jnp.float32)
        power = lag_real * lag_real + lag_imag * lag_imag
        w_real = jnp.concatenate([lag_real * power, lag_real], axis=0).astype(jnp.bfloat16)
        w_imag = jnp.concatenate([-lag_imag * power, -lag_imag], axis=0).astype(jnp.bfloat16)
        zed_real = product(steer_real, w_real, last) - product(steer_imag, w_imag, last)
        zed_imag = product(steer_imag, w_real, last) + product(steer_real, w_imag, last)
        y_real = contrib[0].astype(jnp.float32)
        y_imag = contrib[1].astype(jnp.float32)
        term_a = lax.optimization_barrier(jnp.sum(y_real * zed_imag[:, :ROWS_DEV] + y_imag * zed_real[:, :ROWS_DEV], axis=1))
        term_b = lax.optimization_barrier(jnp.sum(y_real * zed_imag[:, ROWS_DEV:] + y_imag * zed_real[:, ROWS_DEV:], axis=1))
        image_tile = jnp.stack([image_real, image_imag]).astype(jnp.bfloat16)
        return (image_tile, term_a, term_b, jnp.sum(power), jnp.sum(power * power))
    tiles, terms_a, terms_b, powers, quartics = lax.map(tile_work, jnp.arange(N_TILE, dtype=jnp.int32))
    image = jnp.transpose(tiles, (1, 0, 2, 3)).reshape(2, ROWS, COLS)
    energy = jnp.sum(powers)
    quartic = jnp.sum(quartics)
    total_a = lax.optimization_barrier(jnp.sum(terms_a, axis=0))
    total_b = lax.optimization_barrier(jnp.sum(terms_b, axis=0))
    npix = ROWS * COLS
    factor = -4.0 * npix * math.sqrt(npix)
    phase_gradient = factor / (energy * energy) * (total_a - quartic / energy * total_b)
    return (image, phase_gradient)
```

```python
import functools
import math

import jax
import jax.numpy as jnp
from jax import lax
from jax.experimental import pallas as pl
from jax.experimental.pallas import tpu as pltpu
from jax.sharding import PartitionSpec as P

PB = 8
WMAX = 4
OFFMAX = 12
LANE = 128


def project_kernel(offsets, widths, visible, phases, data, low, high, out):
    copies, rows, span = out.shape
    pulses = rows // 2
    blocks = pulses // PB
    chunks = span // LANE
    first = lax.axis_index("pulse") * blocks
    cosine = jnp.cos(phases[...])
    sine = jnp.sin(phases[...])

    def rotate(ref):
        real = ref[0].astype(jnp.float32)
        imag = ref[1].astype(jnp.float32)
        return jnp.concatenate(
            [real * cosine - imag * sine, real * sine + imag * cosine], axis=0
        ).astype(jnp.bfloat16)

    extended = jnp.concatenate([rotate(low), rotate(data), rotate(high)], axis=1)
    windows = jnp.concatenate(
        [extended[:, 2 * LANE * c : 2 * LANE * c + 4 * LANE] for c in range(chunks)], axis=0
    )
    distance = (
        lax.broadcasted_iota(jnp.int32, (4 * LANE, LANE), 0)
        - 2 * lax.broadcasted_iota(jnp.int32, (4 * LANE, LANE), 1)
        - LANE
    )
    row_block = (lax.broadcasted_iota(jnp.int32, (rows, LANE), 0) % pulses) // PB
    scale = jnp.zeros((rows, LANE), jnp.float32)
    bands = []
    for b in range(blocks):
        shift = offsets[first + b]
        breadth = widths[first + b]
        band = jnp.maximum(breadth - jnp.abs(distance - shift), 0)
        bands.append(band.astype(jnp.float32).astype(jnp.bfloat16))
        seen = visible[0, first + b].astype(jnp.float32)
        wide = jnp.full((rows, LANE), breadth, jnp.int32).astype(jnp.float32)
        scale = jnp.where(row_block == b, seen / (wide * wide), scale)
    summed = jnp.dot(
        windows, jnp.concatenate(bands, axis=1), preferred_element_type=jnp.float32
    )
    for c in range(chunks):
        part = summed[c * rows : (c + 1) * rows]
        picked = part[:, :LANE]
        for b in range(1, blocks):
            picked = jnp.where(row_block == b, part[:, b * LANE : (b + 1) * LANE], picked)
        block = (picked * scale).astype(jnp.bfloat16)
        for k in range(copies):
            out[k, :, c * LANE : (c + 1) * LANE] = block


def turn(count, period):
    quarter = period // 4
    quadrant = (count + quarter // 2) // quarter
    x = (count - quadrant * quarter).astype(jnp.float32) * (2.0 * math.pi / period)
    y = x * x
    s = x * (1.0 + y * (-1 / 6 + y * (1 / 120 + y * (-1 / 5040 + y * (1 / 362880)))))
    c = 1.0 + y * (-1 / 2 + y * (1 / 24 + y * (-1 / 720 + y * (1 / 40320))))
    odd = (quadrant & 1) == 1
    cosine = jnp.where(odd, s, c)
    sine = jnp.where(odd, c, s)
    cosine = jnp.where(((quadrant + 1) & 2) == 2, -cosine, cosine)
    sine = jnp.where((quadrant & 2) == 2, -sine, sine)
    return cosine, sine


def slab_kernel(group, period, lagged, tables, slab_a, slab_b, sums):
    rows, wide = tables.shape
    columns = wide // 2
    size = 2 * group

    @pl.when(pl.program_id(0) == 0)
    def _():
        first = lax.axis_index("pulse") * columns
        lane = lax.broadcasted_iota(jnp.int32, (group, LANE), 1)
        local = lax.broadcasted_iota(jnp.int32, (group, LANE), 0)

        def fill(k, carry):
            pulse = k * group + local
            cosine, sine = turn((pulse * (first + lane)) & (period - 1), period)
            step_cos, step_sin = turn((pulse * LANE) & (period - 1), period)
            top = pl.ds(pl.multiple_of(k * size, size), group)
            low = pl.ds(pl.multiple_of(k * size + group, group), group)
            for j in range(columns // LANE):
                one = slice(j * LANE, (j + 1) * LANE)
                two = slice(columns + j * LANE, columns + (j + 1) * LANE)
                cos16 = cosine.astype(jnp.bfloat16)
                sin16 = sine.astype(jnp.bfloat16)
                tables[top, one] = cos16
                tables[low, one] = -sin16
                tables[top, two] = sin16
                tables[low, two] = cos16
                cosine, sine = (
                    cosine * step_cos - sine * step_sin,
                    sine * step_cos + cosine * step_sin,
                )
            return carry

        lax.fori_loop(0, rows // size, fill, 0)
        sums[...] = jnp.zeros_like(sums)

    real = lagged[0].astype(jnp.float32)
    imag = lagged[1].astype(jnp.float32)
    power = real * real + imag * imag
    sums[0:1, :] += jnp.sum(power, axis=0, keepdims=True)
    sums[1:2, :] += jnp.sum(power * power, axis=0, keepdims=True)
    weighted = jnp.concatenate([real * power, imag * power], axis=1).astype(jnp.bfloat16)
    plain = jnp.concatenate([lagged[0], lagged[1]], axis=1)
    weights = jnp.concatenate([weighted, plain], axis=0)
    count = weighted.shape[0]
    slab = lax.dot_general(
        tables[...], weights, (((1,), (1,)), ((), ())), preferred_element_type=jnp.float32
    )
    slab_a[...] = slab[:, :count]
    slab_b[...] = slab[:, count:]


def term_kernel(group, contrib, slab_a, slab_b, sums, out):
    energy = jnp.sum(sums[0:1, :], axis=1, keepdims=True)
    quartic = jnp.sum(sums[1:2, :], axis=1, keepdims=True)
    lane = lax.broadcasted_iota(jnp.int32, (group, LANE), 1)
    local = lax.broadcasted_iota(jnp.int32, (group, LANE), 0)
    lanes = lax.broadcasted_iota(jnp.int32, (1, LANE), 1)
    tail = jnp.where(lanes == 2 * group, energy, 0.0) + jnp.where(
        lanes == 2 * group + 1, quartic, 0.0
    )
    size = 2 * group
    for k in range(contrib.shape[0]):
        real = contrib[k, :group].astype(jnp.float32)
        imag = contrib[k, group:].astype(jnp.float32)
        row = tail
        for place, slab in ((0, slab_a), (group, slab_b)):
            top = slab[k * size : k * size + group]
            low = slab[k * size + group : (k + 1) * size]
            term = jnp.sum(imag * top - real * low, axis=1, keepdims=True)
            row = row + jnp.sum(
                jnp.where(lane == local + place, term, 0.0), axis=0, keepdims=True
            )
        for t in range(out.shape[0]):
            out[t, k : k + 1, :] = row


def image_kernel(contrib, tables, out):
    rows = contrib.shape[0] * contrib.shape[1]
    left = contrib[...].reshape(rows, contrib.shape[2])
    out[0] = lax.dot_general(
        left, tables[...], (((0,), (0,)), ((), ())), preferred_element_type=jnp.float32
    ).astype(jnp.bfloat16)


def shards(pulse_data, phases, offsets, widths, visible, lagged):
    pulses = pulse_data.shape[1]
    bins = pulse_data.shape[2]
    rows = lagged.shape[1]
    columns = lagged.shape[2]
    n_pulse = lax.axis_size("pulse")
    n_tile = lax.axis_size("tile")
    size = 2 * pulses
    period = columns * n_pulse
    forward = [(i, i + 1) for i in range(n_tile - 1)]
    backward = [(i + 1, i) for i in range(n_tile - 1)]
    low = lax.ppermute(pulse_data[:, :, bins - LANE :], "tile", forward)
    high = lax.ppermute(pulse_data[:, :, :LANE], "tile", backward)

    smem = pl.BlockSpec(memory_space=pltpu.SMEM)
    vmem = pl.BlockSpec(memory_space=pltpu.VMEM)
    contrib = pl.pallas_call(
        project_kernel,
        out_shape=jax.ShapeDtypeStruct((n_pulse, size, rows), jnp.bfloat16),
        in_specs=[smem, smem, smem, vmem, vmem, vmem, vmem],
        out_specs=vmem,
        name="project",
        cost_estimate=pl.CostEstimate(flops=2 * 256 * 512 * 512, bytes_accessed=1 << 21, transcendentals=64),
    )(offsets, widths, visible, phases.reshape(pulses, 1), pulse_data, low, high)
    gathered = lax.all_to_all(contrib, "pulse", 0, 0, tiled=True)

    count = LANE
    tables, slab_a, slab_b, sums = pl.pallas_call(
        functools.partial(slab_kernel, pulses, period),
        grid=(rows // count,),
        out_shape=(
            jax.ShapeDtypeStruct((n_pulse * size, 2 * columns), jnp.bfloat16),
            jax.ShapeDtypeStruct((n_pulse * size, rows), jnp.float32),
            jax.ShapeDtypeStruct((n_pulse * size, rows), jnp.float32),
            jax.ShapeDtypeStruct((8, columns), jnp.float32),
        ),
        in_specs=[pl.BlockSpec((2, count, columns), lambda i: (0, i, 0))],
        out_specs=(
            pl.BlockSpec((n_pulse * size, 2 * columns), lambda i: (0, 0)),
            pl.BlockSpec((n_pulse * size, count), lambda i: (0, i)),
            pl.BlockSpec((n_pulse * size, count), lambda i: (0, i)),
            pl.BlockSpec((8, columns), lambda i: (0, 0)),
        ),
        name="slab",
        compiler_params=pltpu.CompilerParams(vmem_limit_bytes=40 << 20),
        cost_estimate=pl.CostEstimate(
            flops=8 * rows * n_pulse * size * columns, bytes_accessed=10 << 20, transcendentals=0
        ),
    )(lagged)

    terms = pl.pallas_call(
        functools.partial(term_kernel, pulses),
        out_shape=jax.ShapeDtypeStruct((n_tile, n_pulse, LANE), jnp.float32),
        in_specs=[vmem] * 4,
        out_specs=vmem,
        name="term",
        compiler_params=pltpu.CompilerParams(vmem_limit_bytes=16 << 20),
        cost_estimate=pl.CostEstimate(flops=1 << 21, bytes_accessed=5 << 20, transcendentals=0),
    )(gathered, slab_a, slab_b, sums)
    spread = lax.all_to_all(
        terms.reshape(n_tile * n_pulse, LANE), ("tile", "pulse"), 0, 0, tiled=True
    )

    width = 2 * LANE
    steps = columns // width
    image = pl.pallas_call(
        image_kernel,
        grid=(2 * steps,),
        out_shape=jax.ShapeDtypeStruct((2, rows, columns), jnp.bfloat16),
        in_specs=[
            pl.BlockSpec((n_pulse, size, rows), lambda i: (0, 0, 0)),
            pl.BlockSpec((n_pulse * size, width), lambda i: (0, i)),
        ],
        out_specs=pl.BlockSpec((1, rows, width), lambda i: (i // steps, 0, i % steps)),
        name="image",
        compiler_params=pltpu.CompilerParams(vmem_limit_bytes=24 << 20),
        cost_estimate=pl.CostEstimate(
            flops=4 * rows * n_pulse * size * columns, bytes_accessed=7 << 20, transcendentals=0
        ),
    )(gathered, tables)

    total = jnp.sum(spread, axis=0)
    term_a = total[:pulses]
    term_b = total[pulses : 2 * pulses]
    energy = total[2 * pulses]
    quartic = total[2 * pulses + 1]
    pixels = rows * n_tile * columns * n_pulse
    factor = -4.0 * pixels * math.sqrt(pixels)
    phase_gradient = factor / (energy * energy) * (term_a - quartic / energy * term_b)
    return (image, phase_gradient)


def solution(mesh):
    return jax.shard_map(
        shards,
        mesh=mesh,
        in_specs=(
            P(None, "pulse", "tile"),
            P("pulse"),
            P(),
            P(),
            P("tile", None),
            P(None, "tile", "pulse"),
        ),
        out_specs=(P(None, "tile", "pulse"), P("pulse")),
        check_vma=False,
    )
```

```python
import functools
import math

import jax
import jax.numpy as jnp
from jax import lax
from jax.experimental import pallas as pl
from jax.experimental.pallas import tpu as pltpu
from jax.sharding import PartitionSpec as P

PB = 8
LANE = 128
EDGE = 8


def group_at(i, half):
    mine = lax.axis_index("pulse") % 2
    return 2 * (i % half) + jnp.where(i < half, mine, 1 - mine)


def lane_iota(shape, dim):
    return lax.broadcasted_iota(jnp.int32, shape, dim)


def column_of(row):
    n = row.shape[1]
    diagonal = lane_iota((n, n), 0) == lane_iota((n, n), 1)
    return jnp.sum(jnp.where(diagonal, row, 0.0), axis=1, keepdims=True)


def project_kernel(offsets, widths, visible, phases, data, out):
    copies = out.shape[0]
    size = 2 * data.shape[1]
    bins = data.shape[2]
    pulses = size // 2
    blocks = pulses // PB
    chunks = bins // 2 // LANE
    first = lax.axis_index("pulse") * blocks
    angle = column_of(phases[...])
    cosine = jnp.cos(angle)
    sine = jnp.sin(angle)
    real = data[0].astype(jnp.float32)
    imag = data[1].astype(jnp.float32)
    phased = jnp.concatenate(
        [real * cosine - imag * sine, real * sine + imag * cosine], axis=0
    ).astype(jnp.bfloat16)
    blank = jnp.zeros((size, LANE), jnp.bfloat16)
    extended = jnp.concatenate([blank, phased, blank], axis=1)
    windows = jnp.concatenate(
        [extended[:, 2 * LANE * c : 2 * LANE * c + 4 * LANE] for c in range(chunks)], axis=0
    )
    distance = lane_iota((4 * LANE, LANE), 0) - 2 * lane_iota((4 * LANE, LANE), 1) - LANE
    row_block = (lane_iota((size, LANE), 0) % pulses) // PB
    scale = jnp.zeros((size, LANE), jnp.float32)
    slot = lane_iota((1, LANE), 1) // (2 * EDGE)
    place = lane_iota((1, LANE), 1) % (2 * EDGE)
    slot_shift = jnp.zeros((1, LANE), jnp.int32)
    slot_width = jnp.ones((1, LANE), jnp.int32)
    bands = []
    for b in range(blocks):
        shift = offsets[first + b]
        breadth = widths[first + b]
        band = jnp.maximum(breadth - jnp.abs(distance - shift), 0)
        bands.append(band.astype(jnp.float32).astype(jnp.bfloat16))
        seen = visible[0, first + b].astype(jnp.float32)
        wide = jnp.full((size, LANE), breadth, jnp.int32).astype(jnp.float32)
        scale = jnp.where(row_block == b, seen / (wide * wide), scale)
        slot_shift = jnp.where(slot % blocks == b, shift, slot_shift)
        slot_width = jnp.where(slot % blocks == b, breadth, slot_width)
    summed = jnp.dot(
        windows, jnp.concatenate(bands, axis=1), preferred_element_type=jnp.float32
    )
    for c in range(chunks):
        part = summed[c * size : (c + 1) * size]
        picked = part[:, :LANE]
        for b in range(1, blocks):
            picked = jnp.where(row_block == b, part[:, b * LANE : (b + 1) * LANE], picked)
        block = (picked * scale).astype(jnp.bfloat16)
        for k in range(copies):
            out[k, c * size : (c + 1) * size, :] = block

    wide = phased.astype(jnp.float32)
    pieces = []
    bands = []
    centre = 2 * (place - EDGE) + slot_shift
    reach = lane_iota((LANE, LANE), 0)
    for s in range(size // PB):
        rows = slice(s * PB, (s + 1) * PB)
        for side in range(2):
            pieces.append(wide[rows, :LANE] if side == 0 else wide[rows, bins - LANE :])
            band = jnp.maximum(slot_width - jnp.abs(reach - centre - side * LANE), 0)
            here = (slot == s) & (place // EDGE == side)
            bands.append(jnp.where(here, band, 0).astype(jnp.float32).astype(jnp.bfloat16))
    edge = jnp.dot(
        jnp.concatenate(pieces, axis=1).astype(jnp.bfloat16),
        jnp.concatenate(bands, axis=0),
        preferred_element_type=jnp.float32,
    )
    wide = slot_width.astype(jnp.float32)
    edge = edge / (wide * wide)
    edge = jnp.concatenate([edge, jnp.zeros_like(edge)], axis=0).astype(jnp.bfloat16)
    for k in range(copies):
        out[k, chunks * size :, :] = edge


def message_kernel(contrib, head, tail, visible, to_next, to_last):
    blocks = visible.shape[1]
    columns = head.shape[2]
    sees = jnp.concatenate(
        [visible[...].astype(jnp.float32), jnp.zeros((1, LANE - blocks), jnp.float32)], axis=1
    )
    note = jnp.concatenate(
        [
            jnp.broadcast_to(sees, (EDGE, LANE)),
            contrib[0].astype(jnp.float32)[:EDGE],
            jnp.zeros((EDGE, columns - 2 * LANE), jnp.float32),
        ],
        axis=1,
    )
    for c in range(2):
        first = head[c].astype(jnp.float32)[:EDGE]
        last = tail[c].astype(jnp.float32)[EDGE:]
        to_last[c] = jnp.concatenate([first, note], axis=0).astype(jnp.bfloat16)
        to_next[c] = jnp.concatenate([last, note], axis=0).astype(jnp.bfloat16)


def unpack_edges(packed, size, target):
    lane = lane_iota((PB, LANE), 1)
    parts = []
    for rows in packed:
        row = rows.astype(jnp.float32)[:PB]
        for s in range(size // PB):
            parts.append(jnp.where(lane // (2 * EDGE) == s, row, 0.0))
    spread = (lane_iota((LANE, LANE), 0) % (2 * EDGE)) == target
    return jnp.dot(
        jnp.concatenate(parts, axis=0).astype(jnp.bfloat16),
        spread.astype(jnp.float32).astype(jnp.bfloat16),
        preferred_element_type=jnp.float32,
    )


def row_mask(table, rows, size):
    blocks = table.shape[0]
    row = lane_iota((rows, blocks), 0)
    per = size // 2 // PB
    hit = group_at(row // size, rows // size // 2) * per + (row % (size // 2)) // PB == lane_iota((rows, blocks), 1)
    return jnp.dot(
        hit.astype(jnp.float32).astype(jnp.bfloat16),
        table.astype(jnp.bfloat16),
        preferred_element_type=jnp.float32,
    )


def turn(count, period):
    quarter = period // 4
    quadrant = (count + quarter // 2) // quarter
    x = (count - quadrant * quarter).astype(jnp.float32) * (2.0 * math.pi / period)
    y = x * x
    s = x * (1.0 + y * (-1 / 6 + y * (1 / 120 + y * (-1 / 5040 + y * (1 / 362880)))))
    c = 1.0 + y * (-1 / 2 + y * (1 / 24 + y * (-1 / 720 + y * (1 / 40320))))
    odd = (quadrant & 1) == 1
    cosine = jnp.where(odd, s, c)
    sine = jnp.where(odd, c, s)
    cosine = jnp.where(((quadrant + 1) & 2) == 2, -cosine, cosine)
    sine = jnp.where((quadrant & 2) == 2, -sine, sine)
    return cosine, sine


def slab_of(tables, real16, imag16):
    real = real16.astype(jnp.float32)
    imag = imag16.astype(jnp.float32)
    power = real * real + imag * imag
    weighted = jnp.concatenate([real * power, imag * power], axis=1).astype(jnp.bfloat16)
    plain = jnp.concatenate([real16, imag16], axis=1)
    slab = lax.dot_general(
        tables[...],
        jnp.concatenate([weighted, plain], axis=0),
        (((1,), (1,)), ((), ())),
        preferred_element_type=jnp.float32,
    )
    return slab[:, :LANE], slab[:, LANE:], power


def slab_kernel(group, period, blocks, lagged, before, after, tables, slab_a, slab_b, sums):
    rows, wide = tables.shape
    columns = wide // 2
    size = 2 * group

    first = lax.axis_index("pulse") * columns
    lane = lane_iota((group, LANE), 1)
    local = lane_iota((group, LANE), 0)

    def fill(k, carry):
        pulse = group_at(k, rows // size // 2) * group + local
        cosine, sine = turn((pulse * (first + lane)) & (period - 1), period)
        step_cos, step_sin = turn((pulse * LANE) & (period - 1), period)
        top = pl.ds(pl.multiple_of(k * size, size), group)
        low = pl.ds(pl.multiple_of(k * size + group, group), group)
        for j in range(columns // LANE):
            one = slice(j * LANE, (j + 1) * LANE)
            two = slice(columns + j * LANE, columns + (j + 1) * LANE)
            cos16 = cosine.astype(jnp.bfloat16)
            sin16 = sine.astype(jnp.bfloat16)
            tables[top, one] = cos16
            tables[low, one] = -sin16
            tables[top, two] = sin16
            tables[low, two] = cos16
            cosine, sine = (
                cosine * step_cos - sine * step_sin,
                sine * step_cos + cosine * step_sin,
            )
        return carry

    lax.fori_loop(0, rows // size, fill, 0)
    sums[...] = jnp.zeros_like(sums)

    def multiply(i, carry):
        here = pl.ds(pl.multiple_of(i * LANE, LANE), LANE)
        slab_a[i], slab_b[i], power = slab_of(
            tables, lagged[0, here, :], lagged[1, here, :]
        )
        sums[0:1, :] += jnp.sum(power, axis=0, keepdims=True)
        sums[1:2, :] += jnp.sum(power * power, axis=0, keepdims=True)
        return carry

    chunks = lagged.shape[1] // LANE
    lax.fori_loop(0, chunks, multiply, 0)

    def edge_rows(c):
        both = [ref[c].astype(jnp.float32)[:EDGE] for ref in (before, after)]
        rest = jnp.zeros((LANE - 2 * EDGE, columns), jnp.float32)
        return jnp.concatenate(both + [rest], axis=0).astype(jnp.bfloat16)

    notes = [ref[0].astype(jnp.float32)[EDGE:] for ref in (before, after)]
    sees = [column_of(note[:1, :LANE])[:blocks] for note in notes]
    place = lane_iota((blocks, LANE), 1)
    seen = jnp.where(place < EDGE, sees[0], jnp.where(place < 2 * EDGE, sees[1], 0.0))
    mask = row_mask(seen, rows, size)
    weighted, plain, _ = slab_of(tables, edge_rows(0), edge_rows(1))
    slab_a[chunks] = weighted * mask
    slab_b[chunks] = plain * mask


def term_kernel(group, near, far, slab_a, slab_b, sums, out):
    energy = jnp.sum(sums[0:1, :], axis=1, keepdims=True)
    quartic = jnp.sum(sums[1:2, :], axis=1, keepdims=True)
    lane = lane_iota((group, LANE), 1)
    local = lane_iota((group, LANE), 0)
    lanes = lax.broadcasted_iota(jnp.int32, (1, LANE), 1)
    tail = jnp.where(lanes == 2 * group, energy, 0.0) + jnp.where(
        lanes == 2 * group + 1, quartic, 0.0
    )
    size = 2 * group
    chunks = slab_a.shape[0] - 1
    half = near.shape[0]
    for k in range(2 * half):
        part = near if k < half else far
        if k % half == 0:
            edges = unpack_edges(
                [part[i, chunks * size :, :] for i in range(half)], size, lane_iota((LANE, LANE), 1)
            )
        row = tail
        for place, slab in ((0, slab_a), (group, slab_b)):
            term = jnp.zeros((group, LANE), jnp.float32)
            for i in range(chunks + 1):
                turned = slab[i, k * size : (k + 1) * size]
                if i < chunks:
                    both = part[k % half, i * size : (i + 1) * size, :].astype(jnp.float32)
                else:
                    both = edges[(k % half) * size : (k % half + 1) * size]
                term = term + (both[group:] * turned[:group] - both[:group] * turned[group:])
            term = jnp.sum(term, axis=1, keepdims=True)
            row = row + jnp.sum(
                jnp.where(lane == local + place, term, 0.0), axis=0, keepdims=True
            )
        for t in range(out.shape[0]):
            out[t, pl.ds(group_at(k, half), 1), :] = row


def edge_kernel(near, far, terms, out):
    half, depth, _ = near.shape
    for i in range(half):
        out[i] = near[i, depth - 2 * EDGE :, :]
        out[half + i] = far[i, depth - 2 * EDGE :, :]


def image_kernel(size, near, far, tables, out):
    rows = tables.shape[0]
    parts = [
        jnp.concatenate(
            [part[:, c * size : (c + 1) * size, :].reshape(rows // 2, LANE) for part in (near, far)]
        )
        for c in range(out.shape[1] // LANE)
    ]
    left = jnp.concatenate(parts, axis=1)
    width = 2 * LANE
    columns = out.shape[2]
    for c in range(2):
        for j in range(columns // width):
            start = c * columns + j * width
            out[c, :, j * width : (j + 1) * width] = lax.dot_general(
                left,
                tables[:, start : start + width],
                (((0,), (0,)), ((), ())),
                preferred_element_type=jnp.float32,
            ).astype(jnp.bfloat16)


def edge_image_kernel(size, chunks, near, far, before, after, visible, tables, image, out, rows32):
    rows, wide = tables.shape
    columns = wide // 2

    @pl.when(pl.program_id(0) == 0)
    def _():
        seen = column_of(visible[...].astype(jnp.float32))
        mask = row_mask(jnp.broadcast_to(seen, (seen.shape[0], LANE)), rows, size)
        target = lane_iota((LANE, LANE), 1)
        low = unpack_edges([before[i] for i in range(before.shape[0])], size, jnp.where(target < EDGE, target + EDGE, -1))
        high = unpack_edges([after[i] for i in range(after.shape[0])], size, target - (LANE - EDGE))
        own = [
            jnp.concatenate(
                [
                    part[:, c * size : (c + 1) * size, :].reshape(rows // 2, LANE)
                    for part in (near, far)
                ]
            ).astype(jnp.float32)
            for c in (0, chunks - 1)
        ]
        lane = lane_iota((rows, LANE), 1)
        own = jnp.where(lane < LANE // 2, own[0], own[1])
        left = (own + (low + high) * mask).astype(jnp.bfloat16)
        rows32[...] = lax.dot_general(
            left, tables[...], (((0,), (0,)), ((), ())), preferred_element_type=jnp.float32
        )

    for side in range(2):
        here = slice(0, 2 * EDGE) if side == 0 else slice(LANE - 2 * EDGE, LANE)

        @pl.when(pl.program_id(0) == side)
        def _():
            for c in range(2):
                out[c] = rows32[here, c * columns : (c + 1) * columns].astype(jnp.bfloat16)


def final_kernel(group, factor, spread, out):
    total = jnp.sum(spread[...], axis=0, keepdims=True)
    lanes = lax.broadcasted_iota(jnp.int32, total.shape, 1)

    def pick(place):
        return jnp.sum(jnp.where(lanes == place, total, 0.0), axis=1, keepdims=True)

    energy = pick(2 * group)
    quartic = pick(2 * group + 1)
    term_b = pltpu.roll(total, LANE - group, 1)
    gradient = (factor / (energy * energy)) * (total - (quartic / energy) * term_b)
    out[...] = gradient[:, :group]


def shards(pulse_data, phases, offsets, widths, visible, lagged):
    pulses = pulse_data.shape[1]
    bins = pulse_data.shape[2]
    rows = lagged.shape[1]
    columns = lagged.shape[2]
    n_pulse = lax.axis_size("pulse")
    n_tile = lax.axis_size("tile")
    size = 2 * pulses
    period = columns * n_pulse
    forward = [(i, i + 1) for i in range(n_tile - 1)]
    backward = [(i + 1, i) for i in range(n_tile - 1)]
    smem = pl.BlockSpec(memory_space=pltpu.SMEM)
    vmem = pl.BlockSpec(memory_space=pltpu.VMEM)
    chunks = rows // LANE
    depth = chunks * size + 2 * EDGE
    contrib = pl.pallas_call(
        project_kernel,
        out_shape=jax.ShapeDtypeStruct((n_pulse // 2, depth, LANE), jnp.bfloat16),
        in_specs=[smem, smem, smem, vmem, vmem],
        out_specs=vmem,
        name="project",
        cost_estimate=pl.CostEstimate(flops=1 << 27, bytes_accessed=1 << 21, transcendentals=64),
    )(offsets, widths, visible, phases.reshape(1, pulses), pulse_data)
    columns_of = [list(range(c, n_pulse, 2)) for c in range(2)]
    near = lax.all_to_all(contrib, "pulse", 0, 0, tiled=True, axis_index_groups=columns_of)

    blocks = visible.shape[1]
    message = jax.ShapeDtypeStruct((2, 2 * EDGE, columns), jnp.bfloat16)
    last = rows // (2 * EDGE) - 1
    to_next, to_last = pl.pallas_call(
        message_kernel,
        grid=(1,),
        out_shape=(message, message),
        in_specs=[
            pl.BlockSpec((1, 2 * EDGE, LANE), lambda i: (0, depth // (2 * EDGE) - 1, 0)),
            pl.BlockSpec((2, 2 * EDGE, columns), lambda i: (0, 0, 0)),
            pl.BlockSpec((2, 2 * EDGE, columns), lambda i: (0, last, 0)),
            pl.BlockSpec(visible.shape, lambda i: (0, 0)),
        ],
        out_specs=(pl.BlockSpec(message.shape, lambda i: (0, 0, 0)),) * 2,
        name="message",
    )(contrib, lagged, lagged, visible)
    before = lax.ppermute(to_next, "tile", forward)
    after = lax.ppermute(to_last, "tile", backward)

    near, own, before, after = lax.optimization_barrier((near, lagged, before, after))
    far = lax.ppermute(near, "pulse", [(i, i ^ 1) for i in range(n_pulse)])
    tables, slab_a, slab_b, sums = pl.pallas_call(
        functools.partial(slab_kernel, pulses, period, blocks),
        out_shape=(
            jax.ShapeDtypeStruct((n_pulse * size, 2 * columns), jnp.bfloat16),
            jax.ShapeDtypeStruct((chunks + 1, n_pulse * size, LANE), jnp.float32),
            jax.ShapeDtypeStruct((chunks + 1, n_pulse * size, LANE), jnp.float32),
            jax.ShapeDtypeStruct((8, columns), jnp.float32),
        ),
        in_specs=[vmem] * 3,
        out_specs=(vmem,) * 4,
        name="slab",
        compiler_params=pltpu.CompilerParams(vmem_limit_bytes=20 << 20),
        cost_estimate=pl.CostEstimate(
            flops=8 * rows * n_pulse * size * columns, bytes_accessed=10 << 20, transcendentals=0
        ),
    )(own, before, after)
    terms = pl.pallas_call(
        functools.partial(term_kernel, pulses),
        out_shape=jax.ShapeDtypeStruct((n_tile, n_pulse, LANE), jnp.float32),
        in_specs=[vmem] * 5,
        out_specs=vmem,
        name="term",
        compiler_params=pltpu.CompilerParams(vmem_limit_bytes=8 << 20),
        cost_estimate=pl.CostEstimate(flops=1 << 21, bytes_accessed=5 << 20, transcendentals=0),
    )(near, far, slab_a, slab_b, sums)
    spread = lax.all_to_all(
        terms.reshape(n_tile * n_pulse, LANE), ("tile", "pulse"), 0, 0, tiled=True
    )

    edges = pl.pallas_call(
        edge_kernel,
        out_shape=jax.ShapeDtypeStruct((n_pulse, 2 * EDGE, LANE), jnp.bfloat16),
        in_specs=[vmem, vmem, pl.BlockSpec(memory_space=pl.ANY)],
        out_specs=vmem,
        name="edge",
        compiler_params=pltpu.CompilerParams(vmem_limit_bytes=4 << 20),
    )(near, far, terms)
    edge_before = lax.ppermute(edges, "tile", forward)
    edge_after = lax.ppermute(edges, "tile", backward)
    image = pl.pallas_call(
        functools.partial(image_kernel, size),
        out_shape=jax.ShapeDtypeStruct((2, rows, columns), jnp.bfloat16),
        in_specs=[vmem] * 3,
        out_specs=vmem,
        name="image",
        compiler_params=pltpu.CompilerParams(vmem_limit_bytes=12 << 20),
        cost_estimate=pl.CostEstimate(
            flops=4 * rows * n_pulse * size * columns, bytes_accessed=7 << 20, transcendentals=0
        ),
    )(near, far, tables)
    image = pl.pallas_call(
        functools.partial(edge_image_kernel, size, chunks),
        grid=(2,),
        out_shape=jax.ShapeDtypeStruct((2, rows, columns), jnp.bfloat16),
        in_specs=[vmem] * 6 + [pl.BlockSpec(memory_space=pl.ANY)],
        out_specs=pl.BlockSpec((2, 2 * EDGE, columns), lambda i: (0, i * last, 0)),
        scratch_shapes=[pltpu.VMEM((LANE, 2 * columns), jnp.float32)],
        input_output_aliases={6: 0},
        name="edge_image",
        compiler_params=pltpu.CompilerParams(vmem_limit_bytes=12 << 20),
        cost_estimate=pl.CostEstimate(flops=1 << 29, bytes_accessed=5 << 20, transcendentals=0),
    )(near, far, edge_before, edge_after, visible, tables, image)

    pixels = rows * n_tile * columns * n_pulse
    factor = -4.0 * pixels * math.sqrt(pixels)
    gradient = pl.pallas_call(
        functools.partial(final_kernel, pulses, factor),
        out_shape=jax.ShapeDtypeStruct((1, pulses), jnp.float32),
        in_specs=[vmem],
        out_specs=vmem,
        name="final",
        compiler_params=pltpu.CompilerParams(vmem_limit_bytes=2 << 20),
    )(spread)
    phase_gradient = gradient.reshape(pulses)
    return (image, phase_gradient)


def solution(mesh):
    return jax.shard_map(
        shards,
        mesh=mesh,
        in_specs=(
            P(None, "pulse", "tile"),
            P("pulse"),
            P(),
            P(),
            P("tile", None),
            P(None, "tile", "pulse"),
        ),
        out_specs=(P(None, "tile", "pulse"), P("pulse")),
        check_vma=False,
    )
```

```python
import functools
import math

import jax
import jax.numpy as jnp
from jax import lax
from jax.experimental import pallas as pl
from jax.experimental.pallas import tpu as pltpu
from jax.sharding import PartitionSpec as P

PB = 8
LANE = 128
EDGE = 8


def group_at(i, half):
    mine = lax.axis_index("pulse") % 2
    return 2 * (i % half) + jnp.where(i < half, mine, 1 - mine)


def sides(twin, other):
    even = lax.axis_index("tile") % 2 == 0
    twin = twin.astype(jnp.float32)
    other = other.astype(jnp.float32)
    return jnp.where(even, other, twin), jnp.where(even, twin, other)


def lane_iota(shape, dim):
    return lax.broadcasted_iota(jnp.int32, shape, dim)


def column_of(row):
    n = row.shape[1]
    diagonal = lane_iota((n, n), 0) == lane_iota((n, n), 1)
    return jnp.sum(jnp.where(diagonal, row, 0.0), axis=1, keepdims=True)


def project_kernel(offsets, widths, visible, phases, data, out):
    copies = out.shape[0]
    size = 2 * data.shape[1]
    bins = data.shape[2]
    pulses = size // 2
    blocks = pulses // PB
    chunks = bins // 2 // LANE
    first = lax.axis_index("pulse") * blocks
    angle = column_of(phases[...])
    cosine = jnp.cos(angle)
    sine = jnp.sin(angle)
    real = data[0].astype(jnp.float32)
    imag = data[1].astype(jnp.float32)
    phased = jnp.concatenate(
        [real * cosine - imag * sine, real * sine + imag * cosine], axis=0
    ).astype(jnp.bfloat16)
    blank = jnp.zeros((size, LANE), jnp.bfloat16)
    extended = jnp.concatenate([blank, phased, blank], axis=1)
    windows = jnp.concatenate(
        [extended[:, 2 * LANE * c : 2 * LANE * c + 4 * LANE] for c in range(chunks)], axis=0
    )
    distance = lane_iota((4 * LANE, LANE), 0) - 2 * lane_iota((4 * LANE, LANE), 1) - LANE
    row_block = (lane_iota((size, LANE), 0) % pulses) // PB
    scale = jnp.zeros((size, LANE), jnp.float32)
    slot = lane_iota((1, LANE), 1) // (2 * EDGE)
    place = lane_iota((1, LANE), 1) % (2 * EDGE)
    slot_shift = jnp.zeros((1, LANE), jnp.int32)
    slot_width = jnp.ones((1, LANE), jnp.int32)
    bands = []
    for b in range(blocks):
        shift = offsets[first + b]
        breadth = widths[first + b]
        band = jnp.maximum(breadth - jnp.abs(distance - shift), 0)
        bands.append(band.astype(jnp.float32).astype(jnp.bfloat16))
        seen = visible[0, first + b].astype(jnp.float32)
        wide = jnp.full((size, LANE), breadth, jnp.int32).astype(jnp.float32)
        scale = jnp.where(row_block == b, seen / (wide * wide), scale)
        slot_shift = jnp.where(slot % blocks == b, shift, slot_shift)
        slot_width = jnp.where(slot % blocks == b, breadth, slot_width)
    summed = jnp.dot(
        windows, jnp.concatenate(bands, axis=1), preferred_element_type=jnp.float32
    )
    for c in range(chunks):
        part = summed[c * size : (c + 1) * size]
        picked = part[:, :LANE]
        for b in range(1, blocks):
            picked = jnp.where(row_block == b, part[:, b * LANE : (b + 1) * LANE], picked)
        block = (picked * scale).astype(jnp.bfloat16)
        for k in range(copies):
            out[k, c * size : (c + 1) * size, :] = block

    wide = phased.astype(jnp.float32)
    pieces = []
    bands = []
    centre = 2 * (place - EDGE) + slot_shift
    reach = lane_iota((LANE, LANE), 0)
    for s in range(size // PB):
        rows = slice(s * PB, (s + 1) * PB)
        for side in range(2):
            pieces.append(wide[rows, :LANE] if side == 0 else wide[rows, bins - LANE :])
            band = jnp.maximum(slot_width - jnp.abs(reach - centre - side * LANE), 0)
            here = (slot == s) & (place // EDGE == side)
            bands.append(jnp.where(here, band, 0).astype(jnp.float32).astype(jnp.bfloat16))
    edge = jnp.dot(
        jnp.concatenate(pieces, axis=1).astype(jnp.bfloat16),
        jnp.concatenate(bands, axis=0),
        preferred_element_type=jnp.float32,
    )
    wide = slot_width.astype(jnp.float32)
    edge = edge / (wide * wide)
    edge = jnp.concatenate([edge, jnp.zeros_like(edge)], axis=0).astype(jnp.bfloat16)
    for k in range(copies):
        out[k, chunks * size :, :] = edge


def message_kernel(contrib, head, tail, visible, to_twin, to_other):
    blocks = visible.shape[1]
    columns = head.shape[2]
    sees = jnp.concatenate(
        [visible[...].astype(jnp.float32), jnp.zeros((1, LANE - blocks), jnp.float32)], axis=1
    )
    note = jnp.concatenate(
        [
            jnp.broadcast_to(sees, (EDGE, LANE)),
            contrib[0].astype(jnp.float32)[:EDGE],
            jnp.zeros((EDGE, columns - 2 * LANE), jnp.float32),
        ],
        axis=1,
    )
    even = lax.axis_index("tile") % 2 == 0
    for c in range(2):
        first = head[c].astype(jnp.float32)[:EDGE]
        last = tail[c].astype(jnp.float32)[EDGE:]
        to_twin[c] = jnp.concatenate([jnp.where(even, last, first), note]).astype(jnp.bfloat16)
        to_other[c] = jnp.concatenate([jnp.where(even, first, last), note]).astype(jnp.bfloat16)


def unpack_edges(packed, size, target):
    lane = lane_iota((PB, LANE), 1)
    parts = []
    for rows in packed:
        row = rows.astype(jnp.float32)[:PB]
        for s in range(size // PB):
            parts.append(jnp.where(lane // (2 * EDGE) == s, row, 0.0))
    spread = (lane_iota((LANE, LANE), 0) % (2 * EDGE)) == target
    return jnp.dot(
        jnp.concatenate(parts, axis=0).astype(jnp.bfloat16),
        spread.astype(jnp.float32).astype(jnp.bfloat16),
        preferred_element_type=jnp.float32,
    )


def row_mask(table, rows, size):
    blocks = table.shape[0]
    row = lane_iota((rows, blocks), 0)
    per = size // 2 // PB
    hit = group_at(row // size, rows // size // 2) * per + (row % (size // 2)) // PB == lane_iota((rows, blocks), 1)
    return jnp.dot(
        hit.astype(jnp.float32).astype(jnp.bfloat16),
        table.astype(jnp.bfloat16),
        preferred_element_type=jnp.float32,
    )


def turn(count, period):
    quarter = period // 4
    quadrant = (count + quarter // 2) // quarter
    x = (count - quadrant * quarter).astype(jnp.float32) * (2.0 * math.pi / period)
    y = x * x
    s = x * (1.0 + y * (-1 / 6 + y * (1 / 120 + y * (-1 / 5040 + y * (1 / 362880)))))
    c = 1.0 + y * (-1 / 2 + y * (1 / 24 + y * (-1 / 720 + y * (1 / 40320))))
    odd = (quadrant & 1) == 1
    cosine = jnp.where(odd, s, c)
    sine = jnp.where(odd, c, s)
    cosine = jnp.where(((quadrant + 1) & 2) == 2, -cosine, cosine)
    sine = jnp.where((quadrant & 2) == 2, -sine, sine)
    return cosine, sine


def slab_of(tables, real16, imag16):
    real = real16.astype(jnp.float32)
    imag = imag16.astype(jnp.float32)
    power = real * real + imag * imag
    weighted = jnp.concatenate([real * power, imag * power], axis=1).astype(jnp.bfloat16)
    plain = jnp.concatenate([real16, imag16], axis=1)
    slab = lax.dot_general(
        tables[...],
        jnp.concatenate([weighted, plain], axis=0),
        (((1,), (1,)), ((), ())),
        preferred_element_type=jnp.float32,
    )
    return slab[:, :LANE], slab[:, LANE:], power


def slab_kernel(group, period, blocks, lagged, twin, other, tables, slab_a, slab_b, sums):
    rows, wide = tables.shape
    columns = wide // 2
    size = 2 * group

    first = lax.axis_index("pulse") * columns
    lane = lane_iota((group, LANE), 1)
    local = lane_iota((group, LANE), 0)

    def fill(k, carry):
        pulse = group_at(k, rows // size // 2) * group + local
        cosine, sine = turn((pulse * (first + lane)) & (period - 1), period)
        step_cos, step_sin = turn((pulse * LANE) & (period - 1), period)
        top = pl.ds(pl.multiple_of(k * size, size), group)
        low = pl.ds(pl.multiple_of(k * size + group, group), group)
        for j in range(columns // LANE):
            one = slice(j * LANE, (j + 1) * LANE)
            two = slice(columns + j * LANE, columns + (j + 1) * LANE)
            cos16 = cosine.astype(jnp.bfloat16)
            sin16 = sine.astype(jnp.bfloat16)
            tables[top, one] = cos16
            tables[low, one] = -sin16
            tables[top, two] = sin16
            tables[low, two] = cos16
            cosine, sine = (
                cosine * step_cos - sine * step_sin,
                sine * step_cos + cosine * step_sin,
            )
        return carry

    lax.fori_loop(0, rows // size, fill, 0)
    sums[...] = jnp.zeros_like(sums)

    def multiply(i, carry):
        here = pl.ds(pl.multiple_of(i * LANE, LANE), LANE)
        slab_a[i], slab_b[i], power = slab_of(
            tables, lagged[0, here, :], lagged[1, here, :]
        )
        sums[0:1, :] += jnp.sum(power, axis=0, keepdims=True)
        sums[1:2, :] += jnp.sum(power * power, axis=0, keepdims=True)
        return carry

    chunks = lagged.shape[1] // LANE
    lax.fori_loop(0, chunks, multiply, 0)

    def edge_rows(c):
        both = [note[:EDGE] for note in sides(twin[c], other[c])]
        rest = jnp.zeros((LANE - 2 * EDGE, columns), jnp.float32)
        return jnp.concatenate(both + [rest], axis=0).astype(jnp.bfloat16)

    sees = [
        column_of(note[EDGE : EDGE + 1, :LANE])[:blocks] for note in sides(twin[0], other[0])
    ]
    place = lane_iota((blocks, LANE), 1)
    seen = jnp.where(place < EDGE, sees[0], jnp.where(place < 2 * EDGE, sees[1], 0.0))
    mask = row_mask(seen, rows, size)
    weighted, plain, _ = slab_of(tables, edge_rows(0), edge_rows(1))
    slab_a[chunks] = weighted * mask
    slab_b[chunks] = plain * mask


def term_kernel(group, near, far, slab_a, slab_b, sums, out):
    energy = jnp.sum(sums[0:1, :], axis=1, keepdims=True)
    quartic = jnp.sum(sums[1:2, :], axis=1, keepdims=True)
    lane = lane_iota((group, LANE), 1)
    local = lane_iota((group, LANE), 0)
    lanes = lax.broadcasted_iota(jnp.int32, (1, LANE), 1)
    tail = jnp.where(lanes == 2 * group, energy, 0.0) + jnp.where(
        lanes == 2 * group + 1, quartic, 0.0
    )
    size = 2 * group
    chunks = slab_a.shape[0] - 1
    half = near.shape[0]
    for k in range(2 * half):
        part = near if k < half else far
        if k % half == 0:
            edges = unpack_edges(
                [part[i, chunks * size :, :] for i in range(half)], size, lane_iota((LANE, LANE), 1)
            )
        row = tail
        for place, slab in ((0, slab_a), (group, slab_b)):
            term = jnp.zeros((group, LANE), jnp.float32)
            for i in range(chunks + 1):
                turned = slab[i, k * size : (k + 1) * size]
                if i < chunks:
                    both = part[k % half, i * size : (i + 1) * size, :].astype(jnp.float32)
                else:
                    both = edges[(k % half) * size : (k % half + 1) * size]
                term = term + (both[group:] * turned[:group] - both[:group] * turned[group:])
            term = jnp.sum(term, axis=1, keepdims=True)
            row = row + jnp.sum(
                jnp.where(lane == local + place, term, 0.0), axis=0, keepdims=True
            )
        for t in range(out.shape[0]):
            out[t, pl.ds(group_at(k, half), 1), :] = row


def edge_kernel(near, far, terms, out):
    half, depth, _ = near.shape
    for i in range(half):
        out[i] = near[i, depth - 2 * EDGE :, :]
        out[half + i] = far[i, depth - 2 * EDGE :, :]


def image_kernel(size, near, far, tables, out):
    rows = tables.shape[0]
    parts = [
        jnp.concatenate(
            [part[:, c * size : (c + 1) * size, :].reshape(rows // 2, LANE) for part in (near, far)]
        )
        for c in range(out.shape[1] // LANE)
    ]
    left = jnp.concatenate(parts, axis=1)
    width = 2 * LANE
    columns = out.shape[2]
    for c in range(2):
        for j in range(columns // width):
            start = c * columns + j * width
            out[c, :, j * width : (j + 1) * width] = lax.dot_general(
                left,
                tables[:, start : start + width],
                (((0,), (0,)), ((), ())),
                preferred_element_type=jnp.float32,
            ).astype(jnp.bfloat16)


def edge_image_kernel(size, chunks, near, far, twin, other, visible, tables, image, out, rows32):
    rows, wide = tables.shape
    columns = wide // 2

    @pl.when(pl.program_id(0) == 0)
    def _():
        seen = column_of(visible[...].astype(jnp.float32))
        mask = row_mask(jnp.broadcast_to(seen, (seen.shape[0], LANE)), rows, size)
        target = lane_iota((LANE, LANE), 1)
        both = [sides(twin[i], other[i]) for i in range(twin.shape[0])]
        low = unpack_edges([pair[0] for pair in both], size, jnp.where(target < EDGE, target + EDGE, -1))
        high = unpack_edges([pair[1] for pair in both], size, target - (LANE - EDGE))
        own = [
            jnp.concatenate(
                [
                    part[:, c * size : (c + 1) * size, :].reshape(rows // 2, LANE)
                    for part in (near, far)
                ]
            ).astype(jnp.float32)
            for c in (0, chunks - 1)
        ]
        lane = lane_iota((rows, LANE), 1)
        own = jnp.where(lane < LANE // 2, own[0], own[1])
        left = (own + (low + high) * mask).astype(jnp.bfloat16)
        rows32[...] = lax.dot_general(
            left, tables[...], (((0,), (0,)), ((), ())), preferred_element_type=jnp.float32
        )

    for side in range(2):
        here = slice(0, 2 * EDGE) if side == 0 else slice(LANE - 2 * EDGE, LANE)

        @pl.when(pl.program_id(0) == side)
        def _():
            for c in range(2):
                out[c] = rows32[here, c * columns : (c + 1) * columns].astype(jnp.bfloat16)


def final_kernel(group, factor, spread, out):
    total = jnp.sum(spread[...], axis=0, keepdims=True)
    lanes = lax.broadcasted_iota(jnp.int32, total.shape, 1)

    def pick(place):
        return jnp.sum(jnp.where(lanes == place, total, 0.0), axis=1, keepdims=True)

    energy = pick(2 * group)
    quartic = pick(2 * group + 1)
    term_b = pltpu.roll(total, LANE - group, 1)
    gradient = (factor / (energy * energy)) * (total - (quartic / energy) * term_b)
    out[...] = gradient[:, :group]


def shards(pulse_data, phases, offsets, widths, visible, lagged):
    pulses = pulse_data.shape[1]
    bins = pulse_data.shape[2]
    rows = lagged.shape[1]
    columns = lagged.shape[2]
    n_pulse = lax.axis_size("pulse")
    n_tile = lax.axis_size("tile")
    size = 2 * pulses
    period = columns * n_pulse
    twins = [(i, i ^ 1) for i in range(n_tile)]
    others = [(i, i + 1 if i % 2 else i - 1) for i in range(1, n_tile - 1)]
    smem = pl.BlockSpec(memory_space=pltpu.SMEM)
    vmem = pl.BlockSpec(memory_space=pltpu.VMEM)
    chunks = rows // LANE
    depth = chunks * size + 2 * EDGE
    contrib = pl.pallas_call(
        project_kernel,
        out_shape=jax.ShapeDtypeStruct((n_pulse // 2, depth, LANE), jnp.bfloat16),
        in_specs=[smem, smem, smem, vmem, vmem],
        out_specs=vmem,
        name="project",
        cost_estimate=pl.CostEstimate(flops=1 << 27, bytes_accessed=1 << 21, transcendentals=64),
    )(offsets, widths, visible, phases.reshape(1, pulses), pulse_data)
    columns_of = [list(range(c, n_pulse, 2)) for c in range(2)]
    near = lax.all_to_all(contrib, "pulse", 0, 0, tiled=True, axis_index_groups=columns_of)

    blocks = visible.shape[1]
    message = jax.ShapeDtypeStruct((2, 2 * EDGE, columns), jnp.bfloat16)
    last = rows // (2 * EDGE) - 1
    to_twin, to_other = pl.pallas_call(
        message_kernel,
        grid=(1,),
        out_shape=(message, message),
        in_specs=[
            pl.BlockSpec((1, 2 * EDGE, LANE), lambda i: (0, depth // (2 * EDGE) - 1, 0)),
            pl.BlockSpec((2, 2 * EDGE, columns), lambda i: (0, 0, 0)),
            pl.BlockSpec((2, 2 * EDGE, columns), lambda i: (0, last, 0)),
            pl.BlockSpec(visible.shape, lambda i: (0, 0)),
        ],
        out_specs=(pl.BlockSpec(message.shape, lambda i: (0, 0, 0)),) * 2,
        name="message",
    )(contrib, lagged, lagged, visible)
    twin = lax.ppermute(to_twin, "tile", twins)
    other = lax.ppermute(to_other, "tile", others)

    near, own, twin, other = lax.optimization_barrier((near, lagged, twin, other))
    far = lax.ppermute(near, "pulse", [(i, i ^ 1) for i in range(n_pulse)])
    tables, slab_a, slab_b, sums = pl.pallas_call(
        functools.partial(slab_kernel, pulses, period, blocks),
        out_shape=(
            jax.ShapeDtypeStruct((n_pulse * size, 2 * columns), jnp.bfloat16),
            jax.ShapeDtypeStruct((chunks + 1, n_pulse * size, LANE), jnp.float32),
            jax.ShapeDtypeStruct((chunks + 1, n_pulse * size, LANE), jnp.float32),
            jax.ShapeDtypeStruct((8, columns), jnp.float32),
        ),
        in_specs=[vmem] * 3,
        out_specs=(vmem,) * 4,
        name="slab",
        compiler_params=pltpu.CompilerParams(vmem_limit_bytes=20 << 20),
        cost_estimate=pl.CostEstimate(
            flops=8 * rows * n_pulse * size * columns, bytes_accessed=10 << 20, transcendentals=0
        ),
    )(own, twin, other)
    terms = pl.pallas_call(
        functools.partial(term_kernel, pulses),
        out_shape=jax.ShapeDtypeStruct((n_tile, n_pulse, LANE), jnp.float32),
        in_specs=[vmem] * 5,
        out_specs=vmem,
        name="term",
        compiler_params=pltpu.CompilerParams(vmem_limit_bytes=8 << 20),
        cost_estimate=pl.CostEstimate(flops=1 << 21, bytes_accessed=5 << 20, transcendentals=0),
    )(near, far, slab_a, slab_b, sums)
    spread = lax.all_to_all(
        terms.reshape(n_tile * n_pulse, LANE), ("tile", "pulse"), 0, 0, tiled=True
    )

    edges = pl.pallas_call(
        edge_kernel,
        out_shape=jax.ShapeDtypeStruct((n_pulse, 2 * EDGE, LANE), jnp.bfloat16),
        in_specs=[vmem, vmem, pl.BlockSpec(memory_space=pl.ANY)],
        out_specs=vmem,
        name="edge",
        compiler_params=pltpu.CompilerParams(vmem_limit_bytes=4 << 20),
    )(near, far, terms)
    edge_twin = lax.ppermute(edges, "tile", twins)
    edge_other = lax.ppermute(edges, "tile", others)
    image = pl.pallas_call(
        functools.partial(image_kernel, size),
        out_shape=jax.ShapeDtypeStruct((2, rows, columns), jnp.bfloat16),
        in_specs=[vmem] * 3,
        out_specs=vmem,
        name="image",
        compiler_params=pltpu.CompilerParams(vmem_limit_bytes=12 << 20),
        cost_estimate=pl.CostEstimate(
            flops=4 * rows * n_pulse * size * columns, bytes_accessed=7 << 20, transcendentals=0
        ),
    )(near, far, tables)
    image = pl.pallas_call(
        functools.partial(edge_image_kernel, size, chunks),
        grid=(2,),
        out_shape=jax.ShapeDtypeStruct((2, rows, columns), jnp.bfloat16),
        in_specs=[vmem] * 6 + [pl.BlockSpec(memory_space=pl.ANY)],
        out_specs=pl.BlockSpec((2, 2 * EDGE, columns), lambda i: (0, i * last, 0)),
        scratch_shapes=[pltpu.VMEM((LANE, 2 * columns), jnp.float32)],
        input_output_aliases={6: 0},
        name="edge_image",
        compiler_params=pltpu.CompilerParams(vmem_limit_bytes=12 << 20),
        cost_estimate=pl.CostEstimate(flops=1 << 29, bytes_accessed=5 << 20, transcendentals=0),
    )(near, far, edge_twin, edge_other, visible, tables, image)

    pixels = rows * n_tile * columns * n_pulse
    factor = -4.0 * pixels * math.sqrt(pixels)
    gradient = pl.pallas_call(
        functools.partial(final_kernel, pulses, factor),
        out_shape=jax.ShapeDtypeStruct((1, pulses), jnp.float32),
        in_specs=[vmem],
        out_specs=vmem,
        name="final",
        compiler_params=pltpu.CompilerParams(vmem_limit_bytes=2 << 20),
    )(spread)
    phase_gradient = gradient.reshape(pulses)
    return (image, phase_gradient)


def solution(mesh):
    return jax.shard_map(
        shards,
        mesh=mesh,
        in_specs=(
            P(None, "pulse", "tile"),
            P("pulse"),
            P(),
            P(),
            P("tile", None),
            P(None, "tile", "pulse"),
        ),
        out_specs=(P(None, "tile", "pulse"), P("pulse")),
        check_vma=False,
    )
```

```python
import functools
import math

import jax
import jax.numpy as jnp
from jax import lax
from jax.experimental import pallas as pl
from jax.experimental.pallas import tpu as pltpu
from jax.sharding import PartitionSpec as P

PB = 8
LANE = 128
EDGE = 8


def line_order(i, count):
    return jnp.where(i < count // 2, 2 * i, 2 * count - 1 - 2 * i)


def group_at(i, half):
    mine = lax.axis_index("pulse") % 2
    return 2 * line_order(i % half, half) + jnp.where(i < half, mine, 1 - mine)


def sides(twin, other):
    even = lax.axis_index("tile") % 2 == 0
    twin = twin.astype(jnp.float32)
    other = other.astype(jnp.float32)
    return jnp.where(even, other, twin), jnp.where(even, twin, other)


def lane_iota(shape, dim):
    return lax.broadcasted_iota(jnp.int32, shape, dim)


def column_of(row):
    n = row.shape[1]
    diagonal = lane_iota((n, n), 0) == lane_iota((n, n), 1)
    return jnp.sum(jnp.where(diagonal, row, 0.0), axis=1, keepdims=True)


def project_kernel(offsets, widths, visible, phases, data, out, message, sent):
    copies = out.shape[0]
    size = 2 * data.shape[1]
    bins = data.shape[2]
    pulses = size // 2
    blocks = pulses // PB
    chunks = bins // 2 // LANE
    first = lax.axis_index("pulse") * blocks
    angle = column_of(phases[...])
    cosine = jnp.cos(angle)
    sine = jnp.sin(angle)
    real = data[0].astype(jnp.float32)
    imag = data[1].astype(jnp.float32)
    phased = jnp.concatenate(
        [real * cosine - imag * sine, real * sine + imag * cosine], axis=0
    ).astype(jnp.bfloat16)
    blank = jnp.zeros((size, LANE), jnp.bfloat16)
    extended = jnp.concatenate([blank, phased, blank], axis=1)
    windows = jnp.concatenate(
        [extended[:, 2 * LANE * c : 2 * LANE * c + 4 * LANE] for c in range(chunks)], axis=0
    )
    distance = lane_iota((4 * LANE, LANE), 0) - 2 * lane_iota((4 * LANE, LANE), 1) - LANE
    row_block = (lane_iota((size, LANE), 0) % pulses) // PB
    scale = jnp.zeros((size, LANE), jnp.float32)
    slot = lane_iota((1, LANE), 1) // (2 * EDGE)
    place = lane_iota((1, LANE), 1) % (2 * EDGE)
    slot_shift = jnp.zeros((1, LANE), jnp.int32)
    slot_width = jnp.ones((1, LANE), jnp.int32)
    bands = []
    for b in range(blocks):
        shift = offsets[first + b]
        breadth = widths[first + b]
        band = jnp.maximum(breadth - jnp.abs(distance - shift), 0)
        bands.append(band.astype(jnp.float32).astype(jnp.bfloat16))
        seen = visible[0, first + b].astype(jnp.float32)
        wide = jnp.full((size, LANE), breadth, jnp.int32).astype(jnp.float32)
        scale = jnp.where(row_block == b, seen / (wide * wide), scale)
        slot_shift = jnp.where(slot % blocks == b, shift, slot_shift)
        slot_width = jnp.where(slot % blocks == b, breadth, slot_width)
    summed = jnp.dot(
        windows, jnp.concatenate(bands, axis=1), preferred_element_type=jnp.float32
    )
    for c in range(chunks):
        part = summed[c * size : (c + 1) * size]
        picked = part[:, :LANE]
        for b in range(1, blocks):
            picked = jnp.where(row_block == b, part[:, b * LANE : (b + 1) * LANE], picked)
        block = (picked * scale).astype(jnp.bfloat16)
        message[c * size : (c + 1) * size, :] = block

    wide = phased.astype(jnp.float32)
    pieces = []
    bands = []
    centre = 2 * (place - EDGE) + slot_shift
    reach = lane_iota((LANE, LANE), 0)
    for s in range(size // PB):
        rows = slice(s * PB, (s + 1) * PB)
        for side in range(2):
            pieces.append(wide[rows, :LANE] if side == 0 else wide[rows, bins - LANE :])
            band = jnp.maximum(slot_width - jnp.abs(reach - centre - side * LANE), 0)
            here = (slot == s) & (place // EDGE == side)
            bands.append(jnp.where(here, band, 0).astype(jnp.float32).astype(jnp.bfloat16))
    edge = jnp.dot(
        jnp.concatenate(pieces, axis=1).astype(jnp.bfloat16),
        jnp.concatenate(bands, axis=0),
        preferred_element_type=jnp.float32,
    )
    wide = slot_width.astype(jnp.float32)
    edge = edge / (wide * wide)
    edge = jnp.concatenate([edge, jnp.zeros_like(edge)], axis=0).astype(jnp.bfloat16)
    message[chunks * size :, :] = edge
    sends = [pltpu.make_async_copy(message, out.at[k], sent.at[k]) for k in range(copies)]
    for send in sends:
        send.start()
    for send in sends:
        send.wait()


def message_kernel(contrib, head, tail, visible, to_twin, to_other):
    blocks = visible.shape[1]
    columns = head.shape[2]
    sees = jnp.concatenate(
        [visible[...].astype(jnp.float32), jnp.zeros((1, LANE - blocks), jnp.float32)], axis=1
    )
    note = jnp.concatenate(
        [
            jnp.broadcast_to(sees, (EDGE, LANE)),
            contrib[0].astype(jnp.float32)[:EDGE],
            jnp.zeros((EDGE, columns - 2 * LANE), jnp.float32),
        ],
        axis=1,
    )
    even = lax.axis_index("tile") % 2 == 0
    for c in range(2):
        first = head[c].astype(jnp.float32)[:EDGE]
        last = tail[c].astype(jnp.float32)[EDGE:]
        to_twin[c] = jnp.concatenate([jnp.where(even, last, first), note]).astype(jnp.bfloat16)
        to_other[c] = jnp.concatenate([jnp.where(even, first, last), note]).astype(jnp.bfloat16)


def unpack_edges(packed, size, target):
    lane = lane_iota((PB, LANE), 1)
    parts = []
    for rows in packed:
        row = rows.astype(jnp.float32)[:PB]
        for s in range(size // PB):
            parts.append(jnp.where(lane // (2 * EDGE) == s, row, 0.0))
    spread = (lane_iota((LANE, LANE), 0) % (2 * EDGE)) == target
    return jnp.dot(
        jnp.concatenate(parts, axis=0).astype(jnp.bfloat16),
        spread.astype(jnp.float32).astype(jnp.bfloat16),
        preferred_element_type=jnp.float32,
    )


def row_mask(table, rows, size):
    blocks = table.shape[0]
    row = lane_iota((rows, blocks), 0)
    per = size // 2 // PB
    hit = group_at(row // size, rows // size // 2) * per + (row % (size // 2)) // PB == lane_iota((rows, blocks), 1)
    return jnp.dot(
        hit.astype(jnp.float32).astype(jnp.bfloat16),
        table.astype(jnp.bfloat16),
        preferred_element_type=jnp.float32,
    )


def turn(count, period):
    quarter = period // 4
    quadrant = (count + quarter // 2) // quarter
    x = (count - quadrant * quarter).astype(jnp.float32) * (2.0 * math.pi / period)
    y = x * x
    s = x * (1.0 + y * (-1 / 6 + y * (1 / 120 + y * (-1 / 5040 + y * (1 / 362880)))))
    c = 1.0 + y * (-1 / 2 + y * (1 / 24 + y * (-1 / 720 + y * (1 / 40320))))
    odd = (quadrant & 1) == 1
    cosine = jnp.where(odd, s, c)
    sine = jnp.where(odd, c, s)
    cosine = jnp.where(((quadrant + 1) & 2) == 2, -cosine, cosine)
    sine = jnp.where((quadrant & 2) == 2, -sine, sine)
    return cosine, sine


def slab_of(tables, real16, imag16):
    real = real16.astype(jnp.float32)
    imag = imag16.astype(jnp.float32)
    power = real * real + imag * imag
    weighted = jnp.concatenate([real * power, imag * power], axis=1).astype(jnp.bfloat16)
    plain = jnp.concatenate([real16, imag16], axis=1)
    slab = lax.dot_general(
        tables[...],
        jnp.concatenate([weighted, plain], axis=0),
        (((1,), (1,)), ((), ())),
        preferred_element_type=jnp.float32,
    )
    return slab[:, :LANE], slab[:, LANE:], power


def slab_kernel(group, period, blocks, lagged, twin, other, tables, slab_a, slab_b, sums):
    rows, wide = tables.shape
    columns = wide // 2
    size = 2 * group

    first = lax.axis_index("pulse") * columns
    lane = lane_iota((group, LANE), 1)
    local = lane_iota((group, LANE), 0)

    def fill(k, carry):
        pulse = group_at(k, rows // size // 2) * group + local
        cosine, sine = turn((pulse * (first + lane)) & (period - 1), period)
        step_cos, step_sin = turn((pulse * LANE) & (period - 1), period)
        top = pl.ds(pl.multiple_of(k * size, size), group)
        low = pl.ds(pl.multiple_of(k * size + group, group), group)
        for j in range(columns // LANE):
            one = slice(j * LANE, (j + 1) * LANE)
            two = slice(columns + j * LANE, columns + (j + 1) * LANE)
            cos16 = cosine.astype(jnp.bfloat16)
            sin16 = sine.astype(jnp.bfloat16)
            tables[top, one] = cos16
            tables[low, one] = -sin16
            tables[top, two] = sin16
            tables[low, two] = cos16
            cosine, sine = (
                cosine * step_cos - sine * step_sin,
                sine * step_cos + cosine * step_sin,
            )
        return carry

    lax.fori_loop(0, rows // size, fill, 0)
    sums[...] = jnp.zeros_like(sums)

    def multiply(i, carry):
        here = pl.ds(pl.multiple_of(i * LANE, LANE), LANE)
        slab_a[i], slab_b[i], power = slab_of(
            tables, lagged[0, here, :], lagged[1, here, :]
        )
        sums[0:1, :] += jnp.sum(power, axis=0, keepdims=True)
        sums[1:2, :] += jnp.sum(power * power, axis=0, keepdims=True)
        return carry

    chunks = lagged.shape[1] // LANE
    lax.fori_loop(0, chunks, multiply, 0)

    def edge_rows(c):
        both = [note[:EDGE] for note in sides(twin[c], other[c])]
        rest = jnp.zeros((LANE - 2 * EDGE, columns), jnp.float32)
        return jnp.concatenate(both + [rest], axis=0).astype(jnp.bfloat16)

    sees = [
        column_of(note[EDGE : EDGE + 1, :LANE])[:blocks] for note in sides(twin[0], other[0])
    ]
    place = lane_iota((blocks, LANE), 1)
    seen = jnp.where(place < EDGE, sees[0], jnp.where(place < 2 * EDGE, sees[1], 0.0))
    mask = row_mask(seen, rows, size)
    weighted, plain, _ = slab_of(tables, edge_rows(0), edge_rows(1))
    slab_a[chunks] = weighted * mask
    slab_b[chunks] = plain * mask


def term_kernel(group, near, far, slab_a, slab_b, sums, out, rows):
    energy = jnp.sum(sums[0:1, :], axis=1, keepdims=True)
    quartic = jnp.sum(sums[1:2, :], axis=1, keepdims=True)
    lane = lane_iota((group, LANE), 1)
    local = lane_iota((group, LANE), 0)
    lanes = lax.broadcasted_iota(jnp.int32, (1, LANE), 1)
    tail = jnp.where(lanes == 2 * group, energy, 0.0) + jnp.where(
        lanes == 2 * group + 1, quartic, 0.0
    )
    size = 2 * group
    chunks = slab_a.shape[0] - 1
    half = near.shape[0]
    for k in range(2 * half):
        part = near if k < half else far
        if k % half == 0:
            edges = unpack_edges(
                [part[i, chunks * size :, :] for i in range(half)], size, lane_iota((LANE, LANE), 1)
            )
        row = tail
        for place, slab in ((0, slab_a), (group, slab_b)):
            term = jnp.zeros((group, LANE), jnp.float32)
            for i in range(chunks + 1):
                turned = slab[i, k * size : (k + 1) * size]
                if i < chunks:
                    both = part[k % half, i * size : (i + 1) * size, :].astype(jnp.float32)
                else:
                    both = edges[(k % half) * size : (k % half + 1) * size]
                term = term + (both[group:] * turned[:group] - both[:group] * turned[group:])
            term = jnp.sum(term, axis=1, keepdims=True)
            row = row + jnp.sum(
                jnp.where(lane == local + place, term, 0.0), axis=0, keepdims=True
            )
        rows[pl.ds(group_at(k, half), 1), :] = row
    for t in range(out.shape[0]):
        out[t] = rows[...]


def edge_kernel(part, sums, out):
    for i in range(out.shape[0]):
        out[i] = part[i, part.shape[1] - 2 * EDGE :, :]


def inward_kernel(twin, other, terms, out):
    high = lane_iota((2 * EDGE, LANE), 1) % (2 * EDGE) >= EDGE
    for i in range(out.shape[0]):
        before, after = sides(twin[i], other[i])
        out[i] = jnp.where(high, before, after).astype(jnp.bfloat16)


def image_kernel(size, near, far, inward, far_inward, visible, tables, out):
    rows = tables.shape[0]
    seen = column_of(visible[...].astype(jnp.float32))
    mask = row_mask(jnp.broadcast_to(seen, (seen.shape[0], LANE)), rows, size)
    target = lane_iota((LANE, LANE), 1)
    packed = [part[i] for part in (inward, far_inward) for i in range(part.shape[0])]
    low = unpack_edges(packed, size, jnp.where(target < EDGE, target + EDGE, -1))
    high = unpack_edges(packed, size, target - (LANE - EDGE))
    parts = [
        jnp.concatenate(
            [part[:, c * size : (c + 1) * size, :].reshape(rows // 2, LANE) for part in (near, far)]
        )
        for c in range(out.shape[1] // LANE)
    ]
    parts[0] = (parts[0].astype(jnp.float32) + low * mask).astype(jnp.bfloat16)
    parts[-1] = (parts[-1].astype(jnp.float32) + high * mask).astype(jnp.bfloat16)
    left = jnp.concatenate(parts, axis=1)
    width = 2 * LANE
    columns = out.shape[2]
    for c in range(2):
        for j in range(columns // width):
            start = c * columns + j * width
            out[c, :, j * width : (j + 1) * width] = lax.dot_general(
                left,
                tables[:, start : start + width],
                (((0,), (0,)), ((), ())),
                preferred_element_type=jnp.float32,
            ).astype(jnp.bfloat16)


def final_kernel(group, factor, spread, out):
    total = jnp.sum(spread[...], axis=0, keepdims=True)
    lanes = lax.broadcasted_iota(jnp.int32, total.shape, 1)

    def pick(place):
        return jnp.sum(jnp.where(lanes == place, total, 0.0), axis=1, keepdims=True)

    energy = pick(2 * group)
    quartic = pick(2 * group + 1)
    term_b = pltpu.roll(total, LANE - group, 1)
    gradient = (factor / (energy * energy)) * (total - (quartic / energy) * term_b)
    out[...] = gradient[:, :group]


def shards(pulse_data, phases, offsets, widths, visible, lagged):
    pulses = pulse_data.shape[1]
    bins = pulse_data.shape[2]
    rows = lagged.shape[1]
    columns = lagged.shape[2]
    n_pulse = lax.axis_size("pulse")
    n_tile = lax.axis_size("tile")
    size = 2 * pulses
    period = columns * n_pulse
    twins = [(i, i ^ 1) for i in range(n_tile)]
    others = [(i, i + 1 if i % 2 else i - 1) for i in range(1, n_tile - 1)]
    smem = pl.BlockSpec(memory_space=pltpu.SMEM)
    vmem = pl.BlockSpec(memory_space=pltpu.VMEM)
    chunks = rows // LANE
    depth = chunks * size + 2 * EDGE
    contrib = pl.pallas_call(
        project_kernel,
        out_shape=jax.ShapeDtypeStruct((n_pulse // 2, depth, LANE), jnp.bfloat16),
        in_specs=[smem, smem, smem, vmem, vmem],
        out_specs=pl.BlockSpec(memory_space=pltpu.HBM),
        scratch_shapes=[
            pltpu.VMEM((depth, LANE), jnp.bfloat16),
            pltpu.SemaphoreType.DMA((n_pulse // 2,)),
        ],
        name="project",
        cost_estimate=pl.CostEstimate(flops=1 << 27, bytes_accessed=1 << 21, transcendentals=64),
    )(offsets, widths, visible, phases.reshape(1, pulses), pulse_data)
    line = list(range(0, n_pulse // 2, 2)) + list(range(n_pulse // 2 - 1, 0, -2))
    columns_of = [[2 * z + c for z in line] for c in range(2)]
    near = lax.all_to_all(contrib, "pulse", 0, 0, tiled=True, axis_index_groups=columns_of)

    blocks = visible.shape[1]
    message = jax.ShapeDtypeStruct((2, 2 * EDGE, columns), jnp.bfloat16)
    last = rows // (2 * EDGE) - 1
    to_twin, to_other = pl.pallas_call(
        message_kernel,
        grid=(1,),
        out_shape=(message, message),
        in_specs=[
            pl.BlockSpec((1, 2 * EDGE, LANE), lambda i: (0, depth // (2 * EDGE) - 1, 0)),
            pl.BlockSpec((2, 2 * EDGE, columns), lambda i: (0, 0, 0)),
            pl.BlockSpec((2, 2 * EDGE, columns), lambda i: (0, last, 0)),
            pl.BlockSpec(visible.shape, lambda i: (0, 0)),
        ],
        out_specs=(pl.BlockSpec(message.shape, lambda i: (0, 0, 0)),) * 2,
        name="message",
    )(contrib, lagged, lagged, visible)
    twin = lax.ppermute(to_twin, "tile", twins)
    other = lax.ppermute(to_other, "tile", others)

    near, own, twin, other = lax.optimization_barrier((near, lagged, twin, other))
    far = lax.ppermute(near, "pulse", [(i, i ^ 1) for i in range(n_pulse)])
    tables, slab_a, slab_b, sums = pl.pallas_call(
        functools.partial(slab_kernel, pulses, period, blocks),
        out_shape=(
            jax.ShapeDtypeStruct((n_pulse * size, 2 * columns), jnp.bfloat16),
            jax.ShapeDtypeStruct((chunks + 1, n_pulse * size, LANE), jnp.float32),
            jax.ShapeDtypeStruct((chunks + 1, n_pulse * size, LANE), jnp.float32),
            jax.ShapeDtypeStruct((8, columns), jnp.float32),
        ),
        in_specs=[vmem] * 3,
        out_specs=(vmem,) * 4,
        name="slab",
        compiler_params=pltpu.CompilerParams(vmem_limit_bytes=20 << 20),
        cost_estimate=pl.CostEstimate(
            flops=8 * rows * n_pulse * size * columns, bytes_accessed=10 << 20, transcendentals=0
        ),
    )(own, twin, other)
    edge_shape = jax.ShapeDtypeStruct((n_pulse // 2, 2 * EDGE, LANE), jnp.bfloat16)
    edges = pl.pallas_call(
        edge_kernel,
        out_shape=edge_shape,
        in_specs=[vmem, pl.BlockSpec(memory_space=pl.ANY)],
        out_specs=vmem,
        name="edge",
        compiler_params=pltpu.CompilerParams(vmem_limit_bytes=4 << 20),
    )(near, sums)
    edge_twin = lax.ppermute(edges, "tile", twins)
    edge_other = lax.ppermute(edges, "tile", others)
    terms = pl.pallas_call(
        functools.partial(term_kernel, pulses),
        out_shape=jax.ShapeDtypeStruct((n_tile, n_pulse, LANE), jnp.float32),
        in_specs=[vmem] * 5,
        out_specs=vmem,
        scratch_shapes=[pltpu.VMEM((n_pulse, LANE), jnp.float32)],
        name="term",
        compiler_params=pltpu.CompilerParams(vmem_limit_bytes=8 << 20),
        cost_estimate=pl.CostEstimate(flops=1 << 21, bytes_accessed=5 << 20, transcendentals=0),
    )(near, far, slab_a, slab_b, sums)
    spread = lax.all_to_all(
        terms.reshape(n_tile * n_pulse, LANE), ("tile", "pulse"), 0, 0, tiled=True
    )

    inward = pl.pallas_call(
        inward_kernel,
        out_shape=edge_shape,
        in_specs=[vmem, vmem, pl.BlockSpec(memory_space=pl.ANY)],
        out_specs=vmem,
        name="inward",
        compiler_params=pltpu.CompilerParams(vmem_limit_bytes=4 << 20),
    )(edge_twin, edge_other, terms)
    far_inward = lax.ppermute(inward, "pulse", [(i, i ^ 1) for i in range(n_pulse)])
    image = pl.pallas_call(
        functools.partial(image_kernel, size),
        out_shape=jax.ShapeDtypeStruct((2, rows, columns), jnp.bfloat16),
        in_specs=[vmem] * 6,
        out_specs=vmem,
        name="image",
        compiler_params=pltpu.CompilerParams(vmem_limit_bytes=12 << 20),
        cost_estimate=pl.CostEstimate(
            flops=4 * rows * n_pulse * size * columns, bytes_accessed=7 << 20, transcendentals=0
        ),
    )(near, far, inward, far_inward, visible, tables)
    pixels = rows * n_tile * columns * n_pulse
    factor = -4.0 * pixels * math.sqrt(pixels)
    gradient = pl.pallas_call(
        functools.partial(final_kernel, pulses, factor),
        out_shape=jax.ShapeDtypeStruct((1, pulses), jnp.float32),
        in_specs=[vmem],
        out_specs=vmem,
        name="final",
        compiler_params=pltpu.CompilerParams(vmem_limit_bytes=2 << 20),
    )(spread)
    phase_gradient = gradient.reshape(pulses)
    return (image, phase_gradient)


def solution(mesh):
    return jax.shard_map(
        shards,
        mesh=mesh,
        in_specs=(
            P(None, "pulse", "tile"),
            P("pulse"),
            P(),
            P(),
            P("tile", None),
            P(None, "tile", "pulse"),
        ),
        out_specs=(P(None, "tile", "pulse"), P("pulse")),
        check_vma=False,
    )
```

```python
import functools
import math

import jax
import jax.numpy as jnp
from jax import lax
from jax.experimental import pallas as pl
from jax.experimental.pallas import tpu as pltpu
from jax.sharding import PartitionSpec as P

PB = 8
LANE = 128
EDGE = 8


def line_order(i, count):
    return jnp.where(i < count // 2, 2 * i, 2 * count - 1 - 2 * i)


def group_at(i, half):
    mine = lax.axis_index("pulse") % 2
    return 2 * line_order(i % half, half) + jnp.where(i < half, mine, 1 - mine)


def sides(twin, other):
    even = lax.axis_index("tile") % 2 == 0
    twin = twin.astype(jnp.float32)
    other = other.astype(jnp.float32)
    return jnp.where(even, other, twin), jnp.where(even, twin, other)


def lane_iota(shape, dim):
    return lax.broadcasted_iota(jnp.int32, shape, dim)


def column_of(row):
    n = row.shape[1]
    diagonal = lane_iota((n, n), 0) == lane_iota((n, n), 1)
    return jnp.sum(jnp.where(diagonal, row, 0.0), axis=1, keepdims=True)


def project_kernel(offsets, widths, visible, phases, data, out, message, sent):
    copies = out.shape[0]
    size = 2 * data.shape[1]
    bins = data.shape[2]
    pulses = size // 2
    blocks = pulses // PB
    chunks = bins // 2 // LANE
    first = lax.axis_index("pulse") * blocks
    angle = column_of(phases[...])
    cosine = jnp.cos(angle)
    sine = jnp.sin(angle)
    real = data[0].astype(jnp.float32)
    imag = data[1].astype(jnp.float32)
    phased = jnp.concatenate(
        [real * cosine - imag * sine, real * sine + imag * cosine], axis=0
    ).astype(jnp.bfloat16)
    blank = jnp.zeros((size, LANE), jnp.bfloat16)
    extended = jnp.concatenate([blank, phased, blank], axis=1)
    windows = jnp.concatenate(
        [extended[:, 2 * LANE * c : 2 * LANE * c + 4 * LANE] for c in range(chunks)], axis=0
    )
    distance = lane_iota((4 * LANE, LANE), 0) - 2 * lane_iota((4 * LANE, LANE), 1) - LANE
    row_block = (lane_iota((size, LANE), 0) % pulses) // PB
    scale = jnp.zeros((size, LANE), jnp.float32)
    slot = lane_iota((1, LANE), 1) // (2 * EDGE)
    place = lane_iota((1, LANE), 1) % (2 * EDGE)
    slot_shift = jnp.zeros((1, LANE), jnp.int32)
    slot_width = jnp.ones((1, LANE), jnp.int32)
    bands = []
    for b in range(blocks):
        shift = offsets[first + b]
        breadth = widths[first + b]
        band = jnp.maximum(breadth - jnp.abs(distance - shift), 0)
        bands.append(band.astype(jnp.float32).astype(jnp.bfloat16))
        seen = visible[0, first + b].astype(jnp.float32)
        wide = jnp.full((size, LANE), breadth, jnp.int32).astype(jnp.float32)
        scale = jnp.where(row_block == b, seen / (wide * wide), scale)
        slot_shift = jnp.where(slot % blocks == b, shift, slot_shift)
        slot_width = jnp.where(slot % blocks == b, breadth, slot_width)
    summed = jnp.dot(
        windows, jnp.concatenate(bands, axis=1), preferred_element_type=jnp.float32
    )
    for c in range(chunks):
        part = summed[c * size : (c + 1) * size]
        picked = part[:, :LANE]
        for b in range(1, blocks):
            picked = jnp.where(row_block == b, part[:, b * LANE : (b + 1) * LANE], picked)
        block = (picked * scale).astype(jnp.bfloat16)
        message[c * size : (c + 1) * size, :] = block

    wide = phased.astype(jnp.float32)
    pieces = []
    bands = []
    centre = 2 * (place - EDGE) + slot_shift
    reach = lane_iota((LANE, LANE), 0)
    for s in range(size // PB):
        rows = slice(s * PB, (s + 1) * PB)
        for side in range(2):
            pieces.append(wide[rows, :LANE] if side == 0 else wide[rows, bins - LANE :])
            band = jnp.maximum(slot_width - jnp.abs(reach - centre - side * LANE), 0)
            here = (slot == s) & (place // EDGE == side)
            bands.append(jnp.where(here, band, 0).astype(jnp.float32).astype(jnp.bfloat16))
    edge = jnp.dot(
        jnp.concatenate(pieces, axis=1).astype(jnp.bfloat16),
        jnp.concatenate(bands, axis=0),
        preferred_element_type=jnp.float32,
    )
    wide = slot_width.astype(jnp.float32)
    edge = edge / (wide * wide)
    edge = jnp.concatenate([edge, jnp.zeros_like(edge)], axis=0).astype(jnp.bfloat16)
    message[chunks * size :, :] = edge
    sends = [pltpu.make_async_copy(message, out.at[k], sent.at[k]) for k in range(copies)]
    for send in sends:
        send.start()
    for send in sends:
        send.wait()


def message_kernel(contrib, head, tail, visible, to_twin, to_other):
    blocks = visible.shape[1]
    columns = head.shape[2]
    sees = jnp.concatenate(
        [visible[...].astype(jnp.float32), jnp.zeros((1, LANE - blocks), jnp.float32)], axis=1
    )
    note = jnp.concatenate(
        [
            jnp.broadcast_to(sees, (EDGE, LANE)),
            contrib[0].astype(jnp.float32)[:EDGE],
            jnp.zeros((EDGE, columns - 2 * LANE), jnp.float32),
        ],
        axis=1,
    )
    even = lax.axis_index("tile") % 2 == 0
    for c in range(2):
        first = head[c].astype(jnp.float32)[:EDGE]
        last = tail[c].astype(jnp.float32)[EDGE:]
        to_twin[c] = jnp.concatenate([jnp.where(even, last, first), note]).astype(jnp.bfloat16)
        to_other[c] = jnp.concatenate([jnp.where(even, first, last), note]).astype(jnp.bfloat16)


def unpack_edges(packed, size, target):
    lane = lane_iota((PB, LANE), 1)
    parts = []
    for rows in packed:
        row = rows.astype(jnp.float32)[:PB]
        for s in range(size // PB):
            parts.append(jnp.where(lane // (2 * EDGE) == s, row, 0.0))
    spread = (lane_iota((LANE, LANE), 0) % (2 * EDGE)) == target
    return jnp.dot(
        jnp.concatenate(parts, axis=0).astype(jnp.bfloat16),
        spread.astype(jnp.float32).astype(jnp.bfloat16),
        preferred_element_type=jnp.float32,
    )


def row_mask(table, rows, size):
    blocks = table.shape[0]
    row = lane_iota((rows, blocks), 0)
    per = size // 2 // PB
    hit = group_at(row // size, rows // size // 2) * per + (row % (size // 2)) // PB == lane_iota((rows, blocks), 1)
    return jnp.dot(
        hit.astype(jnp.float32).astype(jnp.bfloat16),
        table.astype(jnp.bfloat16),
        preferred_element_type=jnp.float32,
    )


def turn(count, period):
    quarter = period // 4
    quadrant = (count + quarter // 2) // quarter
    x = (count - quadrant * quarter).astype(jnp.float32) * (2.0 * math.pi / period)
    y = x * x
    s = x * (1.0 + y * (-1 / 6 + y * (1 / 120 + y * (-1 / 5040 + y * (1 / 362880)))))
    c = 1.0 + y * (-1 / 2 + y * (1 / 24 + y * (-1 / 720 + y * (1 / 40320))))
    odd = (quadrant & 1) == 1
    cosine = jnp.where(odd, s, c)
    sine = jnp.where(odd, c, s)
    cosine = jnp.where(((quadrant + 1) & 2) == 2, -cosine, cosine)
    sine = jnp.where((quadrant & 2) == 2, -sine, sine)
    return cosine, sine


def slab_of(tables, real16, imag16):
    real = real16.astype(jnp.float32)
    imag = imag16.astype(jnp.float32)
    power = real * real + imag * imag
    weighted = jnp.concatenate([real * power, imag * power], axis=1).astype(jnp.bfloat16)
    plain = jnp.concatenate([real16, imag16], axis=1)
    slab = lax.dot_general(
        tables[...],
        jnp.concatenate([weighted, plain], axis=0),
        (((1,), (1,)), ((), ())),
        preferred_element_type=jnp.float32,
    )
    return slab[:, :LANE], slab[:, LANE:], power


def slab_kernel(group, period, blocks, lagged, twin, other, tables, slab_a, slab_b, sums):
    rows, wide = tables.shape
    columns = wide // 2
    size = 2 * group

    first = lax.axis_index("pulse") * columns
    lane = lane_iota((group, LANE), 1)
    local = lane_iota((group, LANE), 0)

    def fill(k, carry):
        pulse = group_at(k, rows // size // 2) * group + local
        cosine, sine = turn((pulse * (first + lane)) & (period - 1), period)
        step_cos, step_sin = turn((pulse * LANE) & (period - 1), period)
        top = pl.ds(pl.multiple_of(k * size, size), group)
        low = pl.ds(pl.multiple_of(k * size + group, group), group)
        for j in range(columns // LANE):
            one = slice(j * LANE, (j + 1) * LANE)
            two = slice(columns + j * LANE, columns + (j + 1) * LANE)
            cos16 = cosine.astype(jnp.bfloat16)
            sin16 = sine.astype(jnp.bfloat16)
            tables[top, one] = cos16
            tables[low, one] = -sin16
            tables[top, two] = sin16
            tables[low, two] = cos16
            cosine, sine = (
                cosine * step_cos - sine * step_sin,
                sine * step_cos + cosine * step_sin,
            )
        return carry

    lax.fori_loop(0, rows // size, fill, 0)
    sums[...] = jnp.zeros_like(sums)

    def multiply(i, carry):
        here = pl.ds(pl.multiple_of(i * LANE, LANE), LANE)
        slab_a[i], slab_b[i], power = slab_of(
            tables, lagged[0, here, :], lagged[1, here, :]
        )
        sums[0:1, :] += jnp.sum(power, axis=0, keepdims=True)
        sums[1:2, :] += jnp.sum(power * power, axis=0, keepdims=True)
        return carry

    chunks = lagged.shape[1] // LANE
    lax.fori_loop(0, chunks, multiply, 0)

    def edge_rows(c):
        both = [note[:EDGE] for note in sides(twin[c], other[c])]
        rest = jnp.zeros((LANE - 2 * EDGE, columns), jnp.float32)
        return jnp.concatenate(both + [rest], axis=0).astype(jnp.bfloat16)

    sees = [
        column_of(note[EDGE : EDGE + 1, :LANE])[:blocks] for note in sides(twin[0], other[0])
    ]
    place = lane_iota((blocks, LANE), 1)
    seen = jnp.where(place < EDGE, sees[0], jnp.where(place < 2 * EDGE, sees[1], 0.0))
    mask = row_mask(seen, rows, size)
    weighted, plain, _ = slab_of(tables, edge_rows(0), edge_rows(1))
    slab_a[chunks] = weighted * mask
    slab_b[chunks] = plain * mask


def term_kernel(group, near, far, slab_a, slab_b, sums, out, rows):
    energy = jnp.sum(sums[0:1, :], axis=1, keepdims=True)
    quartic = jnp.sum(sums[1:2, :], axis=1, keepdims=True)
    lane = lane_iota((group, LANE), 1)
    local = lane_iota((group, LANE), 0)
    lanes = lax.broadcasted_iota(jnp.int32, (1, LANE), 1)
    tail = jnp.where(lanes == 2 * group, energy, 0.0) + jnp.where(
        lanes == 2 * group + 1, quartic, 0.0
    )
    size = 2 * group
    chunks = slab_a.shape[0] - 1
    half = near.shape[0]
    for k in range(2 * half):
        part = near if k < half else far
        if k % half == 0:
            edges = unpack_edges(
                [part[i, chunks * size :, :] for i in range(half)], size, lane_iota((LANE, LANE), 1)
            )
        row = tail
        for place, slab in ((0, slab_a), (group, slab_b)):
            term = jnp.zeros((group, LANE), jnp.float32)
            for i in range(chunks + 1):
                turned = slab[i, k * size : (k + 1) * size]
                if i < chunks:
                    both = part[k % half, i * size : (i + 1) * size, :].astype(jnp.float32)
                else:
                    both = edges[(k % half) * size : (k % half + 1) * size]
                term = term + (both[group:] * turned[:group] - both[:group] * turned[group:])
            term = jnp.sum(term, axis=1, keepdims=True)
            row = row + jnp.sum(
                jnp.where(lane == local + place, term, 0.0), axis=0, keepdims=True
            )
        rows[pl.ds(group_at(k, half), 1), :] = row
    for t in range(out.shape[0]):
        out[t] = rows[...]


def edge_kernel(part, out):
    for i in range(out.shape[0]):
        out[i] = part[i, part.shape[1] - 2 * EDGE :, :]


def inward_kernel(twin, other, terms, out):
    high = lane_iota((2 * EDGE, LANE), 1) % (2 * EDGE) >= EDGE
    for i in range(out.shape[0]):
        before, after = sides(twin[i], other[i])
        out[i] = jnp.where(high, before, after).astype(jnp.bfloat16)


def image_kernel(size, near, far, inward, far_inward, visible, tables, out):
    rows = tables.shape[0]
    seen = column_of(visible[...].astype(jnp.float32))
    mask = row_mask(jnp.broadcast_to(seen, (seen.shape[0], LANE)), rows, size)
    target = lane_iota((LANE, LANE), 1)
    packed = [part[i] for part in (inward, far_inward) for i in range(part.shape[0])]
    low = unpack_edges(packed, size, jnp.where(target < EDGE, target + EDGE, -1))
    high = unpack_edges(packed, size, target - (LANE - EDGE))
    parts = [
        jnp.concatenate(
            [part[:, c * size : (c + 1) * size, :].reshape(rows // 2, LANE) for part in (near, far)]
        )
        for c in range(out.shape[1] // LANE)
    ]
    parts[0] = (parts[0].astype(jnp.float32) + low * mask).astype(jnp.bfloat16)
    parts[-1] = (parts[-1].astype(jnp.float32) + high * mask).astype(jnp.bfloat16)
    left = jnp.concatenate(parts, axis=1)
    width = 2 * LANE
    columns = out.shape[2]
    for c in range(2):
        for j in range(columns // width):
            start = c * columns + j * width
            out[c, :, j * width : (j + 1) * width] = lax.dot_general(
                left,
                tables[:, start : start + width],
                (((0,), (0,)), ((), ())),
                preferred_element_type=jnp.float32,
            ).astype(jnp.bfloat16)


def final_kernel(group, factor, spread, out):
    total = jnp.sum(spread[...], axis=0, keepdims=True)
    lanes = lax.broadcasted_iota(jnp.int32, total.shape, 1)

    def pick(place):
        return jnp.sum(jnp.where(lanes == place, total, 0.0), axis=1, keepdims=True)

    energy = pick(2 * group)
    quartic = pick(2 * group + 1)
    term_b = pltpu.roll(total, LANE - group, 1)
    gradient = (factor / (energy * energy)) * (total - (quartic / energy) * term_b)
    out[...] = gradient[:, :group]


def shards(pulse_data, phases, offsets, widths, visible, lagged):
    pulses = pulse_data.shape[1]
    bins = pulse_data.shape[2]
    rows = lagged.shape[1]
    columns = lagged.shape[2]
    n_pulse = lax.axis_size("pulse")
    n_tile = lax.axis_size("tile")
    size = 2 * pulses
    period = columns * n_pulse
    twins = [(i, i ^ 1) for i in range(n_tile)]
    others = [(i, i + 1 if i % 2 else i - 1) for i in range(1, n_tile - 1)]
    smem = pl.BlockSpec(memory_space=pltpu.SMEM)
    vmem = pl.BlockSpec(memory_space=pltpu.VMEM)
    chunks = rows // LANE
    depth = chunks * size + 2 * EDGE
    contrib = pl.pallas_call(
        project_kernel,
        out_shape=jax.ShapeDtypeStruct((n_pulse // 2, depth, LANE), jnp.bfloat16),
        in_specs=[smem, smem, smem, vmem, vmem],
        out_specs=pl.BlockSpec(memory_space=pltpu.HBM),
        scratch_shapes=[
            pltpu.VMEM((depth, LANE), jnp.bfloat16),
            pltpu.SemaphoreType.DMA((n_pulse // 2,)),
        ],
        name="project",
        cost_estimate=pl.CostEstimate(flops=1 << 27, bytes_accessed=1 << 21, transcendentals=64),
    )(offsets, widths, visible, phases.reshape(1, pulses), pulse_data)
    line = list(range(0, n_pulse // 2, 2)) + list(range(n_pulse // 2 - 1, 0, -2))
    columns_of = [[2 * z + c for z in line] for c in range(2)]
    near = lax.all_to_all(contrib, "pulse", 0, 0, tiled=True, axis_index_groups=columns_of)

    blocks = visible.shape[1]
    message = jax.ShapeDtypeStruct((2, 2 * EDGE, columns), jnp.bfloat16)
    last = rows // (2 * EDGE) - 1
    to_twin, to_other = pl.pallas_call(
        message_kernel,
        grid=(1,),
        out_shape=(message, message),
        in_specs=[
            pl.BlockSpec((1, 2 * EDGE, LANE), lambda i: (0, depth // (2 * EDGE) - 1, 0)),
            pl.BlockSpec((2, 2 * EDGE, columns), lambda i: (0, 0, 0)),
            pl.BlockSpec((2, 2 * EDGE, columns), lambda i: (0, last, 0)),
            pl.BlockSpec(visible.shape, lambda i: (0, 0)),
        ],
        out_specs=(pl.BlockSpec(message.shape, lambda i: (0, 0, 0)),) * 2,
        name="message",
    )(contrib, lagged, lagged, visible)
    twin = lax.ppermute(to_twin, "tile", twins)
    other = lax.ppermute(to_other, "tile", others)

    near, own, twin, other = lax.optimization_barrier((near, lagged, twin, other))
    far = lax.ppermute(near, "pulse", [(i, i ^ 1) for i in range(n_pulse)])
    edge_shape = jax.ShapeDtypeStruct((n_pulse // 2, 2 * EDGE, LANE), jnp.bfloat16)
    edges = pl.pallas_call(
        edge_kernel,
        out_shape=edge_shape,
        in_specs=[vmem],
        out_specs=vmem,
        name="edge",
        compiler_params=pltpu.CompilerParams(vmem_limit_bytes=4 << 20),
    )(near)
    edge_twin = lax.ppermute(edges, "tile", twins)
    edge_other = lax.ppermute(edges, "tile", others)
    edge_twin, own = lax.optimization_barrier((edge_twin, own))
    tables, slab_a, slab_b, sums = pl.pallas_call(
        functools.partial(slab_kernel, pulses, period, blocks),
        out_shape=(
            jax.ShapeDtypeStruct((n_pulse * size, 2 * columns), jnp.bfloat16),
            jax.ShapeDtypeStruct((chunks + 1, n_pulse * size, LANE), jnp.float32),
            jax.ShapeDtypeStruct((chunks + 1, n_pulse * size, LANE), jnp.float32),
            jax.ShapeDtypeStruct((8, columns), jnp.float32),
        ),
        in_specs=[vmem] * 3,
        out_specs=(vmem,) * 4,
        name="slab",
        compiler_params=pltpu.CompilerParams(vmem_limit_bytes=20 << 20),
        cost_estimate=pl.CostEstimate(
            flops=8 * rows * n_pulse * size * columns, bytes_accessed=10 << 20, transcendentals=0
        ),
    )(own, twin, other)
    terms = pl.pallas_call(
        functools.partial(term_kernel, pulses),
        out_shape=jax.ShapeDtypeStruct((n_tile, n_pulse, LANE), jnp.float32),
        in_specs=[vmem] * 5,
        out_specs=vmem,
        scratch_shapes=[pltpu.VMEM((n_pulse, LANE), jnp.float32)],
        name="term",
        compiler_params=pltpu.CompilerParams(vmem_limit_bytes=8 << 20),
        cost_estimate=pl.CostEstimate(flops=1 << 21, bytes_accessed=5 << 20, transcendentals=0),
    )(near, far, slab_a, slab_b, sums)
    spread = lax.all_to_all(
        terms.reshape(n_tile * n_pulse, LANE), ("tile", "pulse"), 0, 0, tiled=True
    )

    inward = pl.pallas_call(
        inward_kernel,
        out_shape=edge_shape,
        in_specs=[vmem, vmem, pl.BlockSpec(memory_space=pl.ANY)],
        out_specs=vmem,
        name="inward",
        compiler_params=pltpu.CompilerParams(vmem_limit_bytes=4 << 20),
    )(edge_twin, edge_other, terms)
    far_inward = lax.ppermute(inward, "pulse", [(i, i ^ 1) for i in range(n_pulse)])
    image = pl.pallas_call(
        functools.partial(image_kernel, size),
        out_shape=jax.ShapeDtypeStruct((2, rows, columns), jnp.bfloat16),
        in_specs=[vmem] * 6,
        out_specs=vmem,
        name="image",
        compiler_params=pltpu.CompilerParams(vmem_limit_bytes=12 << 20),
        cost_estimate=pl.CostEstimate(
            flops=4 * rows * n_pulse * size * columns, bytes_accessed=7 << 20, transcendentals=0
        ),
    )(near, far, inward, far_inward, visible, tables)
    pixels = rows * n_tile * columns * n_pulse
    factor = -4.0 * pixels * math.sqrt(pixels)
    gradient = pl.pallas_call(
        functools.partial(final_kernel, pulses, factor),
        out_shape=jax.ShapeDtypeStruct((1, pulses), jnp.float32),
        in_specs=[vmem],
        out_specs=vmem,
        name="final",
        compiler_params=pltpu.CompilerParams(vmem_limit_bytes=2 << 20),
    )(spread)
    phase_gradient = gradient.reshape(pulses)
    return (image, phase_gradient)


def solution(mesh):
    return jax.shard_map(
        shards,
        mesh=mesh,
        in_specs=(
            P(None, "pulse", "tile"),
            P("pulse"),
            P(),
            P(),
            P("tile", None),
            P(None, "tile", "pulse"),
        ),
        out_specs=(P(None, "tile", "pulse"), P("pulse")),
        check_vma=False,
    )
```
